32 devices in a mesh: seq: 8 (over z, y), tp: 4 (over x, core).
Axes of the slice: x: 2, y: 2, z: 4, core: 2. Of those that a mesh axis runs over, the one named last changes fastest.
Arguments:
- patches: bfloat16 [32, 196, 768], P('seq', 'tp'), may hold values from -6 to 6
- cls_tokens: bfloat16 [32, 768], P(('seq', 'tp')), may hold values from -6 to 6
- frame_clip: int32 [32], P('seq'), may hold values from 0 to 2, as said below
- norm_gain: float32 [2, 3, 768], replicated, may hold values from 0.5 to 1.5
- norm_bias: float32 [2, 3, 768], replicated, may hold values from -2 to 2
- w_tqkv: bfloat16 [2, 768, 2304], replicated, may hold values from -0.21875 to 0.21875
- w_tproj: bfloat16 [2, 768, 768], replicated, may hold values from -0.4375 to 0.4375
- w_tfc: bfloat16 [2, 768, 768], replicated, may hold values from -0.21875 to 0.21875
- w_sqkv: bfloat16 [2, 768, 2304], replicated, may hold values from -0.21875 to 0.21875
- w_sproj: bfloat16 [2, 768, 768], replicated, may hold values from -0.875 to 0.875
- w_fc1: bfloat16 [2, 768, 3072], P(None, None, 'tp'), may hold values from -0.21875 to 0.21875
- w_fc2: bfloat16 [2, 3072, 768], P(None, 'tp'), may hold values from -0.109375 to 0.109375
- cot_patches: bfloat16 [32, 196, 768], P('seq', 'tp'), may hold values from -6 to 6
- cot_cls: bfloat16 [32, 768], P(('seq', 'tp')), may hold values from -6 to 6
Outputs:
- out_patches: bfloat16 [32, 196, 768], P('seq', 'tp')
- out_cls: bfloat16 [32, 768], P(('seq', 'tp'))
- grad_patches: float32 [32, 196, 768], P('seq', 'tp')
- grad_cls: float32 [32, 768], P(('seq', 'tp'))
- grad_attn: float32 [2, 768, 6912], P(None, 'seq')
- grad_norm: float32 [2, 6, 768], P(None, None, 'seq')
- grad_fc1: float32 [2, 768, 3072], P(None, 'seq', 'tp')
- grad_fc2: float32 [2, 3072, 768], P(None, 'tp', 'seq')
The draws below stay inside these ranges and needn't reach their ends.
Inputs may be any that keep to these rules, and one draw needn't show every extreme that they name: frame_clip[f] is the clip of frame f; every clip has 8 to 16 frames and one has exactly 16.
All inputs are finite; a program needn't handle non-finite values.
Results may differ from the reference program's by a relative error of at most 0.03.
Values may be sent and summed in bfloat16 or wider, within the bound.
A program may use at most 384 MiB of HBM per device.

```python
from functools import partial
import jax
import jax.numpy as jnp
from jax import lax

D = 768
FF = 3072
HEAD_DIM = 64
P_SIZE = 196
LAYERS = 2
FRAMES = 32
MAXF = 16
N_SEQ = 8


def draw_frame_clip(key, part):
    key = jax.random.fold_in(key, 7)
    key_first, key_second, key_order = jax.random.split(key, 3)
    rest_frames = FRAMES - MAXF
    clip_slots = rest_frames // 8 + 1
    extra_span = MAXF - 16
    first_draw = jax.random.randint(key_first, (clip_slots,), 0, extra_span + 1)
    second_draw = jax.random.randint(key_second, (clip_slots,), 0, extra_span + 1)
    clip_lengths = 8 + first_draw * second_draw // max(extra_span, 1)
    clip_starts = jnp.cumsum(clip_lengths) - clip_lengths
    valid_start = clip_starts <= rest_frames - 8
    frame_index = jnp.arange(rest_frames)
    rest_ids = jnp.sum((clip_starts[None, :] <= frame_index[:, None]) & valid_start[None, :], axis=1).astype(jnp.int32)
    clip_ids = jnp.concatenate([jnp.zeros((MAXF,), jnp.int32), rest_ids])
    slot_index = jnp.arange(FRAMES)
    stride = FRAMES // N_SEQ
    forced = slot_index % stride == 0
    ranking = jax.random.permutation(key_order, FRAMES)
    score_int = jnp.where(forced, slot_index // stride - FRAMES, ranking)
    order = jnp.argsort(score_int, stable=True)
    return jnp.zeros((FRAMES,), jnp.int32).at[order].set(clip_ids)


def block_scale(own_key, dims, cuts, least, largest):
    def one(dim, parts):
        draws = jax.random.uniform(jax.random.fold_in(jax.random.fold_in(own_key, 6), dim), (parts,), jnp.float32, least / len(cuts), largest / len(cuts))
        return jnp.repeat(jnp.exp(draws), dims[dim] // parts).reshape((-1,) + (1,) * (len(dims) - dim - 1))

    factor_of = one(*cuts[0])
    for cut in cuts[1:]:
        factor_of = factor_of * one(*cut)
    return factor_of


def noise(rng, shape, deviation, bound, cuts=(), kind=jnp.bfloat16):
    drawn = deviation * jax.random.normal(rng, shape, jnp.float32)
    if cuts:
        drawn = drawn * block_scale(rng, shape, cuts, -0.22, 0.18)
    return jnp.clip(drawn, -bound, bound).astype(kind)


def setup_inputs(seed: int = 0) -> dict:
    streams_of = jax.random.split(jax.random.key(seed), 15)
    patches = noise(streams_of[0], (FRAMES, P_SIZE, D), 1.0, 6.0, ((0, 8), (1, 4)))
    cls_tokens = noise(streams_of[1], (FRAMES, D), 1.0, 6.0, ((0, 32),))
    frame_clip = draw_frame_clip(jax.random.fold_in(streams_of[14], 71), 0)
    norm_gain = jnp.clip(1.0 + 0.1 * jax.random.normal(streams_of[3], (LAYERS, 3, D), jnp.float32), 0.5, 1.5)
    norm_bias = noise(streams_of[4], (LAYERS, 3, D), 0.3, 2.0, (), jnp.float32)
    w_tqkv = noise(streams_of[5], (LAYERS, D, 3 * D), D ** -0.5, 0.21875)
    w_tproj = noise(streams_of[6], (LAYERS, D, D), (D // 4) ** -0.5, 0.4375)
    w_tfc = noise(streams_of[7], (LAYERS, D, D), D ** -0.5, 0.21875)
    w_sqkv = noise(streams_of[8], (LAYERS, D, 3 * D), D ** -0.5, 0.21875)
    w_sproj = noise(streams_of[9], (LAYERS, D, D), (D // 16) ** -0.5, 0.875)
    w_fc1 = noise(streams_of[10], (LAYERS, D, FF), D ** -0.5, 0.21875, ((2, 4),))
    w_fc2 = noise(streams_of[11], (LAYERS, FF, D), FF ** -0.5, 0.109375, ((1, 4),))
    cot_patches = noise(streams_of[12], (FRAMES, P_SIZE, D), 1.0, 6.0, ((0, 8), (1, 4)))
    cot_cls = noise(streams_of[13], (FRAMES, D), 1.0, 6.0, ((0, 32),))
    return {"patches": patches, "cls_tokens": cls_tokens, "frame_clip": frame_clip, "norm_gain": norm_gain, "norm_bias": norm_bias, "w_tqkv": w_tqkv, "w_tproj": w_tproj, "w_tfc": w_tfc, "w_sqkv": w_sqkv, "w_sproj": w_sproj, "w_fc1": w_fc1, "w_fc2": w_fc2, "cot_patches": cot_patches, "cot_cls": cot_cls}


EPS = 1e-06
NEG_FILL = -1e+30

@jax.custom_vjp
def low(v):
    return lax.optimization_barrier(v.astype(jnp.bfloat16)).astype(jnp.float32)

@jax.custom_vjp
def low_back(v):
    return v

def low_keep(v):
    return (low(v), None)

def low_pass(kept, grad):
    return (grad,)

def back_keep(v):
    return (v, None)

def back_low(kept, grad):
    return (low(grad),)
low.defvjp(low_keep, low_pass)
low_back.defvjp(back_keep, back_low)

def layer_norm(inputs, gain_row, shift_row):
    center = inputs - lax.optimization_barrier(jnp.mean(inputs, -1, keepdims=True))
    spread = lax.optimization_barrier(jnp.mean(center * center, -1, keepdims=True))
    return center * lax.rsqrt(spread + EPS) * gain_row + shift_row

def matmul(left_rows, right_rows):
    return jnp.matmul(left_rows, right_rows, precision=lax.Precision.HIGHEST)

def heads_of(values):
    return values.reshape(values.shape[:-1] + (values.shape[-1] // HEAD_DIM, HEAD_DIM))

def time_patch(qkv_row, same_clip):
    feature_width = qkv_row.shape[-1] // 3
    queries = heads_of(qkv_row[:, :feature_width])
    key_rows = heads_of(qkv_row[:, feature_width:2 * feature_width])
    val_rows = heads_of(qkv_row[:, 2 * feature_width:])
    scores = low_back(jnp.einsum('fhd,ghd->hfg', queries, key_rows, precision=lax.Precision.HIGHEST) * HEAD_DIM ** (-0.5))
    scores = jnp.where(same_clip[None], scores, NEG_FILL)
    attn_prob = jax.nn.softmax(scores, axis=-1)
    attended = jnp.einsum('hfg,ghd->fhd', low(attn_prob), val_rows, precision=lax.Precision.HIGHEST)
    return attended.reshape(attended.shape[0], -1)

def space_frame(qkv_frame):
    feature_width = qkv_frame.shape[-1] // 3
    queries = heads_of(qkv_frame[:, :feature_width])
    key_rows = heads_of(qkv_frame[:, feature_width:2 * feature_width])
    val_rows = heads_of(qkv_frame[:, 2 * feature_width:])
    scores = low_back(jnp.einsum('phd,khd->hpk', queries, key_rows, precision=lax.Precision.HIGHEST) * HEAD_DIM ** (-0.5))
    attn_prob = jax.nn.softmax(scores, axis=-1)
    attended = jnp.einsum('hpk,khd->phd', low(attn_prob), val_rows, precision=lax.Precision.HIGHEST)
    return attended.reshape(attended.shape[0], -1)

def block(in_patch, in_cls, same_clip, gain_rows, shift_rows, t_qkv, t_proj, t_fc, s_qkv, s_proj, up_w, down_w):
    normed = low(layer_norm(in_patch, gain_rows[0], shift_rows[0]))
    qkv_time = low(low_back(matmul(normed, t_qkv)))
    attended = lax.map(jax.checkpoint(partial(time_patch, same_clip=same_clip)), jnp.swapaxes(qkv_time, 0, 1))
    attended = low(low_back(jnp.swapaxes(attended, 0, 1)))
    projected = low(low_back(matmul(attended, t_proj)))
    mid_patch = in_patch + low_back(matmul(projected, t_fc))
    tokens = jnp.concatenate([in_cls[:, None, :], mid_patch], 1)
    normed = low(layer_norm(tokens, gain_rows[1], shift_rows[1]))
    qkv_space = low(low_back(matmul(normed, s_qkv)))
    spatial = low(low_back(lax.map(jax.checkpoint(space_frame), qkv_space)))
    after = tokens + low_back(matmul(spatial, s_proj))
    normed = low(layer_norm(after, gain_rows[2], shift_rows[2]))
    hidden = low(jax.nn.gelu(low_back(matmul(normed, up_w)), approximate=False))
    final = after + low_back(matmul(hidden, down_w))
    return (final[:, 1:], final[:, 0])

def reference(patches, cls_tokens, frame_clip, norm_gain, norm_bias, w_tqkv, w_tproj, w_tfc, w_sqkv, w_sproj, w_fc1, w_fc2, cot_patches, cot_cls):
    same_clip = frame_clip[:, None] == frame_clip[None, :]

    def forward(in_patch, in_cls, gains, shifts, t_qkv, t_proj, t_fc, s_qkv, s_proj, up_w, down_w):
        for layer_idx in range(LAYERS):
            in_patch, in_cls = block(in_patch, in_cls, same_clip, gains[layer_idx], shifts[layer_idx], t_qkv[layer_idx], t_proj[layer_idx], t_fc[layer_idx], s_qkv[layer_idx], s_proj[layer_idx], up_w[layer_idx], down_w[layer_idx])
        return (in_patch, in_cls)
    floats = (patches.astype(jnp.float32), cls_tokens.astype(jnp.float32), norm_gain, norm_bias, w_tqkv.astype(jnp.float32), w_tproj.astype(jnp.float32), w_tfc.astype(jnp.float32), w_sqkv.astype(jnp.float32), w_sproj.astype(jnp.float32), w_fc1.astype(jnp.float32), w_fc2.astype(jnp.float32))
    outputs, pullback = jax.vjp(forward, *floats)
    gradients = pullback((cot_patches.astype(jnp.float32), cot_cls.astype(jnp.float32)))
    grad_attn = jnp.concatenate([gradients[4], gradients[5], gradients[6], gradients[7], gradients[8]], -1)
    grad_norm = jnp.concatenate([gradients[2], gradients[3]], 1)
    return (outputs[0].astype(jnp.bfloat16), outputs[1].astype(jnp.bfloat16), gradients[0], gradients[1], grad_attn, grad_norm, gradients[9], gradients[10])
```

```python
import functools
from collections import namedtuple
from types import SimpleNamespace

import jax
import jax.numpy as jnp
from jax import lax
from jax.experimental import pallas as pl
from jax.experimental.pallas import tpu as pltpu
from jax.sharding import PartitionSpec as P

HEAD_DIM = 64
LAYERS = 2
SLOT = 8
EPS = 1e-06
NEG_FILL = -1e30
MESH = pl.DeviceIdType.MESH
BF = jnp.bfloat16
F32 = jnp.float32
NN = (((1,), (0,)), ((), ()))
NT = (((1,), (1,)), ((), ()))
TN = (((0,), (0,)), ((), ()))
VMEM_LIMIT = 62 * 1024 * 1024
BLOCK = 32

Cfg = namedtuple("Cfg", ["S", "T", "N", "D", "G", "R", "PER", "HS", "ND", "HG", "C", "FW"])


def dot(left, right, dims=NN):
    return lax.dot_general(left, right, dims, preferred_element_type=F32)


def params(cid=None):
    return pltpu.CompilerParams(
        collective_id=cid, has_side_effects=cid is not None, vmem_limit_bytes=VMEM_LIMIT
    )


ANY = pl.BlockSpec(memory_space=pl.ANY)
VM = pl.BlockSpec(memory_space=pltpu.VMEM)


def my_index(cfg):
    return lax.axis_index("seq") * cfg.T + lax.axis_index("tp")


def device(cfg, index):
    return (index // cfg.T, lax.rem(index, cfg.T))


def greet_all(cfg, me):
    barrier = pltpu.get_barrier_semaphore()

    def signal(i, carry):
        pl.semaphore_signal(
            barrier, inc=1, device_id=device(cfg, lax.rem(me + i, cfg.N)), device_id_type=MESH
        )
        return carry

    lax.fori_loop(1, cfg.N, signal, 0)
    pl.semaphore_wait(barrier, cfg.N - 1)


def wait_bytes(ref, sem):
    pltpu.make_async_copy(ref, ref, sem).wait()


def head_pair(ref, rows, width, part, pair):
    start = part * width + pair * 128
    return ref[rows, start : start + 128]


def softmax_rows(query, key, mask):
    scores = jnp.where(mask, dot(query, key, NT), NEG_FILL)
    top = jnp.max(scores, -1, keepdims=True)
    weight = jnp.exp(scores - top)
    return weight * (1.0 / jnp.sum(weight, -1, keepdims=True))


def for_row_blocks(total, step, block):
    if total == step:
        block(0)
    else:

        def body(i, carry):
            block(pl.multiple_of(i * step, step))
            return carry

        lax.fori_loop(0, total // step, body, 0)


def attend(qkv, kcol, krow, write):
    total, width = qkv.shape[0], qkv.shape[1] // 3
    step = total if total <= 256 else 64
    every = slice(0, total)
    lane = lax.broadcasted_iota(jnp.int32, (step, 128), 1) < HEAD_DIM
    zero = jnp.zeros((), BF)

    def block(first):
        rows = pl.ds(first, step)
        mask = kcol[rows, :] == krow[...]
        for pair in range(width // 128):
            query = head_pair(qkv, rows, width, 0, pair) * jnp.asarray(HEAD_DIM**-0.5, BF)
            key = head_pair(qkv, every, width, 1, pair)
            value = head_pair(qkv, every, width, 2, pair)
            prob0 = softmax_rows(jnp.where(lane, query, zero), key, mask).astype(BF)
            prob1 = softmax_rows(jnp.where(lane, zero, query), key, mask).astype(BF)
            write(first, step, pair, jnp.where(lane, dot(prob0, value), dot(prob1, value)))

    for_row_blocks(total, step, block)


def attend_back(qkv, grad, kcol, krow, write, acc, pairs):
    total, width = qkv.shape[0], qkv.shape[1] // 3
    step = total if total <= 256 else 64
    every = slice(0, total)
    lane = lax.broadcasted_iota(jnp.int32, (step, 128), 1) < HEAD_DIM
    lane_all = lax.broadcasted_iota(jnp.int32, (total, 128), 1) < HEAD_DIM
    zero = jnp.zeros((), BF)
    scale = HEAD_DIM**-0.5

    for pair in pairs:

        def block(first, pair=pair):
            rows = pl.ds(first, step)
            mask = kcol[rows, :] == krow[...]
            key = head_pair(qkv, every, width, 1, pair)
            value = head_pair(qkv, every, width, 2, pair)
            query = head_pair(qkv, rows, width, 0, pair) * jnp.asarray(scale, BF)
            out = grad[rows, pair * 128 : pair * 128 + 128]
            dq, dk, dv = [], [], []
            for lower in (True, False):
                own = (lambda v: jnp.where(lane, v, zero)) if lower else (lambda v: jnp.where(lane, zero, v))
                prob = softmax_rows(own(query), key, mask)
                back = dot(own(out), value, NT)
                delta = jnp.sum(prob * back, -1, keepdims=True)
                score = (prob * (back - delta)).astype(BF)
                dq.append(dot(score, key))
                dk.append(dot(score, query, TN))
                dv.append(dot(prob.astype(BF), out, TN))
            write(first, step, 0, pair, jnp.where(lane, dq[0], dq[1]) * scale)
            grad_key, grad_value = jnp.where(lane_all, dk[0], dk[1]), jnp.where(lane_all, dv[0], dv[1])
            if total == step:
                write(0, total, 1, pair, grad_key)
                write(0, total, 2, pair, grad_value)
            else:
                acc[0] += grad_key
                acc[1] += grad_value

        if total > step:
            acc[...] = jnp.zeros(acc.shape, F32)
        for_row_blocks(total, step, block)
        if total > step:
            write(0, total, 1, pair, acc[0])
            write(0, total, 2, pair, acc[1])


def refs_by_name(names, refs):
    return SimpleNamespace(**dict(zip(names, refs, strict=True)))


def call(build, kernel, inputs, outputs, scratch, cid, **fixed):
    def body(*refs):
        kernel(refs_by_name([*inputs, *outputs, *scratch], refs), **fixed)

    results = build(
        body,
        out_shape=[jax.ShapeDtypeStruct(shape, dtype) for shape, dtype, _ in outputs.values()],
        in_specs=[spec for _, spec in inputs.values()],
        out_specs=[spec for _, _, spec in outputs.values()],
        scratch_shapes=list(scratch.values()),
        compiler_params=params(cid),
    )(*[array for array, _ in inputs.values()])
    return dict(zip(outputs, results, strict=True))


def row_blocks(cfg):
    return [slice(first, min(first + BLOCK, cfg.R)) for first in range(0, cfg.R, BLOCK)]


def normalize(x):
    center = x - jnp.mean(x, -1, keepdims=True)
    root = lax.rsqrt(jnp.mean(center * center, -1, keepdims=True) + EPS)
    return center * root, root


def norm_forward(cfg, src, gain, bias, out):
    for rows in row_blocks(cfg):
        value = (normalize(src[rows, :])[0] * gain + bias).astype(BF)
        if len(out.shape) == 2:
            out[rows, :] = value
        else:
            chunks = slice(rows.start // SLOT, rows.stop // SLOT)
            out[chunks] = value.reshape(chunks.stop - chunks.start, SLOT, cfg.D)


def norm_backward(cfg, src, gain, grad_of, total, sums, layer, which):
    by_gain = by_bias = None
    for rows in row_blocks(cfg):
        normal, root = normalize(src[rows, :])
        grad = grad_of(rows)
        scaled = grad * gain
        inner = jnp.mean(scaled * normal, -1, keepdims=True)
        total[rows, :] += root * (scaled - jnp.mean(scaled, -1, keepdims=True) - normal * inner)
        eights = (grad.shape[0] // 8, 8, grad.shape[1])
        one, two = jnp.sum((grad * normal).reshape(eights), 0), jnp.sum(grad.reshape(eights), 0)
        by_gain = one if by_gain is None else by_gain + one
        by_bias = two if by_bias is None else by_bias + two
    at = layer * 6 + which
    sums[at : at + 1, :] = jnp.sum(by_gain, 0, keepdims=True)
    sums[at + 3 : at + 4, :] = jnp.sum(by_bias, 0, keepdims=True)


def patch_rows(cfg, rows):
    row = lax.broadcasted_iota(jnp.int32, (rows.stop - rows.start, 1), 0) + rows.start
    return lax.rem(row, SLOT) < cfg.PER


def to_all(cfg, me, copy_to, only=None):
    def send(i, carry):
        to = lax.rem(me + i, cfg.N)
        if only is None:
            copy_to(to).start()
        else:

            @pl.when(to < only)
            def _():
                copy_to(to).start()

        return carry

    lax.fori_loop(1, cfg.N, send, 0)


def send_copy(cfg, src, dst, send, recv, to):
    return pltpu.make_async_remote_copy(src, dst, send, recv, device_id=device(cfg, to), device_id_type=MESH)


def tp_copy(src, dst, send, recv, rank):
    return pltpu.make_async_remote_copy(src, dst, send, recv, device_id={"tp": rank}, device_id_type=MESH)


def spread(cfg, me, src, dst, send, recv):
    to_all(cfg, me, lambda to: send_copy(cfg, src.at[to], dst.at[me], send, recv, to), cfg.ND)

    @pl.when(me < cfg.ND)
    def _():
        pltpu.make_async_copy(src.at[me], dst.at[me], recv).start()


def spread_sent(cfg, me, src, send):
    @pl.when(me < cfg.ND)
    def _():
        wait_bytes(src.at[pl.ds(0, cfg.ND - 1)], send)

    @pl.when(me >= cfg.ND)
    def _():
        wait_bytes(src, send)


def collect(cfg, me, src, dst, send, recv):
    to_all(cfg, me, lambda to: send_copy(cfg, src.at[to], dst.at[me], send, recv, to))
    pltpu.make_async_copy(src.at[me], dst.at[me], recv).start()


def collect_sent(cfg, me, src, send):
    @pl.when(me < cfg.ND)
    def _():
        wait_bytes(src.at[pl.ds(0, cfg.N - 1)], send)


def left_rows(cfg):
    return cfg.N * SLOT if cfg.HS == 1 else cfg.R


def head_columns(cfg, split, group):
    return (split * cfg.HG + group) * cfg.C


def swap_tp(x, out, sems):
    rank = lax.axis_index("tp")
    ranks = x.shape[0]
    local = pltpu.make_async_copy(x.at[rank], out.at[rank], sems.at[0])
    copies = [
        tp_copy(x.at[rank ^ i], out.at[rank], sems.at[i], sems.at[ranks + i], rank ^ i) for i in range(1, ranks)
    ]
    local.start()
    for copy in copies:
        copy.start()
    return [local, *copies]


def gelu(value):
    return 0.5 * value * (1.0 + lax.erf(value * 0.7071067811865476))


def gelu_slope(value):
    return 0.5 * (1.0 + lax.erf(value * 0.7071067811865476)) + value * jnp.exp(-0.5 * value * value) * 0.3989422804014327


def gather_tp(own, full, sems, work, beside=lambda: None):
    rank = lax.axis_index("tp")
    mate, across, far = rank ^ 1, rank ^ 2, rank ^ 3
    to_across = tp_copy(own, full.at[rank], sems.at[0], sems.at[1], across)
    to_mate = tp_copy(own, full.at[rank], sems.at[2], sems.at[3], mate)
    to_across.start()
    to_mate.start()
    full[rank] = own[...]
    work(rank)
    beside()
    to_mate.wait_recv()
    work(mate)
    beside()
    beside()
    to_across.wait_recv()
    forward = tp_copy(full.at[across], full.at[across], sems.at[4], sems.at[5], mate)
    forward.start()
    work(across)
    beside()
    forward.wait_recv()
    work(far)
    return [to_across, to_mate, forward]


def scatter_tp(part, from_mate, from_across, sems, beside, write, blocks):
    rank = lax.axis_index("tp")
    mate, across, far = rank ^ 1, rank ^ 2, rank ^ 3
    first = tp_copy(part.at[far], from_mate.at[0], sems.at[0], sems.at[1], mate)
    second = tp_copy(part.at[mate], from_mate.at[1], sems.at[2], sems.at[3], mate)
    third = tp_copy(part.at[across], from_across, sems.at[4], sems.at[5], across)
    first.start()
    second.start()
    first.wait_recv()
    part[across] = (part[across].astype(F32) + from_mate[0].astype(F32)).astype(BF)
    third.start()
    beside()
    second.wait_recv()
    third.wait_recv()
    for rows in blocks:
        near = part[rank, rows, :].astype(F32) + from_mate[1, rows, :].astype(F32)
        write(rows, near + from_across[rows, :].astype(F32))
    return [first, second, third]


WEIGHTS = ["tqkv", "tproj", "tfc", "sqkv", "sproj", "up", "down"]


def weight_scratch(cfg):
    D, FW = cfg.D, cfg.FW
    shapes = [(D, 3 * D), (D, D), (D, D), (D, 3 * D), (D, D), (D, FW), (FW, D)]
    return {name: pltpu.VMEM(shape, BF) for name, shape in zip(WEIGHTS, shapes, strict=True)}


class Weights:
    def __init__(self, r):
        self.r, self.open = r, {}

    def load(self, layer, *names):
        for name in names:
            at = WEIGHTS.index(name)
            copy = pltpu.make_async_copy(getattr(self.r, "w_" + name).at[layer], getattr(self.r, name), self.r.w_sems.at[at])
            copy.start()
            self.open[name] = copy

    def get(self, name):
        if name in self.open:
            self.open.pop(name).wait()
        return getattr(self.r, name)


def forward_kernel(r, cfg):
    me = my_index(cfg)
    rank = lax.axis_index("tp")
    rows_t = cfg.N * SLOT
    C3 = 3 * cfg.C
    blocks = row_blocks(cfg)
    weights = Weights(r)
    weights.load(0, *WEIGHTS)
    greet_all(cfg, me)
    swaps = swap_tp(r.patches, r.patch_in, r.swap_sems.at[0])
    swaps_cot = swap_tp(r.cots, r.cot_in, r.swap_sems.at[1])
    to_all(cfg, me, lambda to: send_copy(cfg, r.key, r.keys.at[me], r.key_sems.at[0], r.key_sems.at[1], to))
    pltpu.make_async_copy(r.key, r.keys.at[me], r.key_sems.at[1]).start()
    ends = []
    saves = []

    def save(src, dst):
        copy = pltpu.make_async_copy(src, dst, r.save_sems.at[len(saves)])
        copy.start()
        saves.append(copy)

    for copy in swaps:
        copy.wait()
    own_rows = cfg.R // cfg.T
    for q in range(cfg.T):
        r.x[0, q * own_rows : (q + 1) * own_rows, :] = r.patch_in[q].astype(F32)
    r.x[0, SLOT - 1 : SLOT, :] = r.cls[...].astype(F32)

    for layer in range(LAYERS):
        x, mid, after = r.x.at[layer], r.mid.at[layer], r.after.at[layer]
        att, proj, n1, so = (r.lefts.at[layer, i] for i in range(4))
        left_t = r.left_t.at[layer]
        save(x, r.o_x.at[layer])
        sems = r.time_sems.at[layer]
        gain0, bias0 = r.gain[layer, 0:1, :], r.bias[layer, 0:1, :]
        if cfg.HS == 1:
            sent = r.sent.at[layer]
            norm_forward(cfg, x, gain0, bias0, sent)
            spread(cfg, me, sent, r.got.at[layer], sems.at[0, 0], sems.at[0, 1])
            ends.append(functools.partial(spread_sent, cfg, me, sent, sems.at[0, 0]))
        else:
            norm_forward(cfg, x, gain0, bias0, left_t)
            tqkv = weights.get("tqkv")
            sent = r.sent.at[layer]
            for split in range(cfg.HS):
                first = head_columns(cfg, split, 0)
                for part in range(3):
                    value = dot(left_t[...], tqkv[:, part * cfg.D + first : part * cfg.D + first + cfg.C]).astype(BF)
                    sent[split * cfg.G : (split + 1) * cfg.G, :, part * cfg.C : (part + 1) * cfg.C] = value.reshape(
                        cfg.G, SLOT, cfg.C
                    )
            spread(cfg, me, sent, r.got.at[layer], sems.at[0, 0], sems.at[0, 1])
            ends.append(functools.partial(spread_sent, cfg, me, sent, sems.at[0, 0]))

        if layer == 0:
            wait_bytes(r.keys, r.key_sems.at[1])
            keys = r.keys[...].reshape(rows_t, 128)
            r.kcol[...] = keys[:, 0:1]
            r.krow[...] = jnp.transpose(keys)[0:1, :]
            save(r.kcol, r.o_kcol)
            save(r.krow, r.o_krow)

        tqkv = weights.get("tqkv")

        @pl.when(me < cfg.ND)
        def _(layer=layer, sems=sems, tqkv=tqkv, left_t=left_t):
            wait_bytes(r.got.at[layer], sems.at[0, 1])
            if cfg.HS == 1:
                left_t[...] = r.got[layer].reshape(rows_t, cfg.D)
            else:
                r.flat[layer, 0] = r.got[layer].reshape(rows_t, C3)
            for group in range(cfg.HG):
                flat = r.flat.at[layer, group]
                if cfg.HS == 1:
                    for part in range(3):
                        first = part * cfg.D + group * cfg.C
                        value = dot(left_t[...], tqkv[:, first : first + cfg.C])
                        flat[:, part * cfg.C : (part + 1) * cfg.C] = value.astype(BF)
                reply = r.reply.at[layer, group]

                def write(first, rows, pair, value, reply=reply):
                    chunks, columns = pl.ds(first // SLOT, rows // SLOT), slice(pair * 128, pair * 128 + 128)
                    reply[chunks, :, columns] = value.astype(BF).reshape(rows // SLOT, SLOT, 128)

                attend(flat, r.kcol, r.krow, write)
                collect(cfg, me, reply, r.back.at[layer, group], sems.at[group, 2], sems.at[group, 3])

        if cfg.HS == 1:

            @pl.when(me >= cfg.ND)
            def _(left_t=left_t):
                left_t[...] = jnp.zeros(left_t.shape, BF)

        if layer + 1 < LAYERS:
            weights.load(layer + 1, "tqkv")
        save(left_t, r.o_left_t.at[layer])
        for group in range(cfg.HG):
            ends.append(functools.partial(collect_sent, cfg, me, r.reply.at[layer, group], sems.at[group, 2]))
            save(r.flat.at[layer, group], r.o_flat.at[layer, group])

        tproj = weights.get("tproj")
        for group in range(cfg.HG):
            wait_bytes(r.back.at[layer, group], sems.at[group, 3])
            for split in range(cfg.HS):
                first = head_columns(cfg, split, group)
                value = r.back[layer, group, split * cfg.G : (split + 1) * cfg.G]
                att[:, first : first + cfg.C] = value.reshape(cfg.R, cfg.C)
        proj[...] = dot(att[...], tproj[...]).astype(BF)
        tfc = weights.get("tfc")
        value = dot(proj[...], tfc[...])
        for rows in blocks:
            mid[rows, :] = x[rows, :] + jnp.where(patch_rows(cfg, rows), value[rows, :], 0.0)
        if layer + 1 < LAYERS:
            weights.load(layer + 1, "tproj", "tfc")
        save(mid, r.o_mid.at[layer])
        norm_forward(cfg, mid, r.gain[layer, 1:2, :], r.bias[layer, 1:2, :], n1)
        sqkv = weights.get("sqkv")
        qkv = r.qkv.at[layer]
        for first in range(0, 3 * cfg.D, cfg.D):
            qkv[:, first : first + cfg.D] = dot(n1[...], sqkv[:, first : first + cfg.D]).astype(BF)
        save(qkv, r.o_qkv.at[layer])

        def write(first, rows, pair, value, so=so):
            so[pl.ds(first, rows), pair * 128 : pair * 128 + 128] = value.astype(BF)

        attend(qkv, r.space_col, r.space_row, write)
        value = dot(so[...], weights.get("sproj")[...])
        after[...] = mid[...] + value
        if layer + 1 < LAYERS:
            weights.load(layer + 1, "sqkv", "sproj")
        save(after, r.o_after.at[layer])
        save(r.lefts.at[layer], r.o_lefts.at[layer])
        norm_forward(cfg, after, r.gain[layer, 2:3, :], r.bias[layer, 2:3, :], r.n2)
        full, part = r.full.at[layer], r.part.at[layer % 2]
        up, down = weights.get("up"), weights.get("down")

        def work(q, full=full, part=part, up=up, down=down):
            rows = full[q]
            for first in range(0, cfg.FW, 256):
                columns = slice(first, min(first + 256, cfg.FW))
                r.hidden[:, columns] = gelu(dot(rows, up[:, columns])).astype(BF)
            part[q] = dot(r.hidden[...], down[...]).astype(BF)

        sems = r.tp_sems.at[layer]
        ends += [copy.wait_send for copy in gather_tp(r.n2, full, sems.at[pl.ds(0, 6)], work)]
        save(full, r.o_full.at[layer])

        def write(rows, value, after=after, layer=layer):
            value = after[rows, :] + value
            if layer + 1 < LAYERS:
                r.x[layer + 1, rows, :] = value
            else:
                r.last[rows, :] = value

        ends += [
            copy.wait_send
            for copy in scatter_tp(
                part, r.from_mate.at[layer], r.from_across.at[layer], sems.at[pl.ds(6, 6)], lambda: None, write, blocks
            )
        ]
        if layer + 1 < LAYERS:
            weights.load(layer + 1, "up", "down")
            for wait in ends:
                wait()
            ends.clear()

    for copy in swaps_cot:
        copy.wait()
    for q in range(cfg.T):
        r.grad[q * own_rows : (q + 1) * own_rows, :] = r.cot_in[q].astype(F32)
    r.grad[SLOT - 1 : SLOT, :] = r.cot_cls[...].astype(F32)
    save(r.grad, r.o_grad)
    save(r.last, r.o_last)
    for wait in ends:
        wait()
    wait_bytes(r.keys.at[pl.ds(0, cfg.N - 1)], r.key_sems.at[0])
    for copy in saves:
        copy.wait()


def forward(cfg, arrays, cid):
    D, R, L = cfg.D, cfg.R, LAYERS
    rows_t, C3 = cfg.N * SLOT, 3 * cfg.C
    wide = D if cfg.HS == 1 else C3
    own_rows = R // cfg.T
    names = ["patches", "cots", "key", "cls", "cot_cls", "gain", "bias", "space_col", "space_row"]
    inputs = {name: (arrays[name], VM) for name in names}
    inputs |= {"w_" + name: (arrays["w_" + name], ANY) for name in WEIGHTS}
    outputs = dict(
        o_x=((L, R, D), F32, ANY),
        o_mid=((L, R, D), F32, ANY),
        o_after=((L, R, D), F32, ANY),
        o_lefts=((L, 4, R, D), BF, ANY),
        o_left_t=((L, left_rows(cfg), D), BF, ANY),
        o_flat=((L, cfg.HG, rows_t, C3), BF, ANY),
        o_qkv=((L, R, 3 * D), BF, ANY),
        o_full=((L, cfg.T, R, D), BF, ANY),
        o_kcol=((rows_t, 1), F32, ANY),
        o_krow=((1, rows_t), F32, ANY),
        o_grad=((R, D), F32, ANY),
        o_last=((R, D), F32, ANY),
    )
    scratch = weight_scratch(cfg) | dict(
        patch_in=pltpu.VMEM((cfg.T, own_rows, D), BF),
        cot_in=pltpu.VMEM((cfg.T, own_rows, D), BF),
        keys=pltpu.VMEM((cfg.N, SLOT, 128), F32),
        kcol=pltpu.VMEM((rows_t, 1), F32),
        krow=pltpu.VMEM((1, rows_t), F32),
        x=pltpu.VMEM((L, R, D), F32),
        mid=pltpu.VMEM((L, R, D), F32),
        after=pltpu.VMEM((L, R, D), F32),
        last=pltpu.VMEM((R, D), F32),
        grad=pltpu.VMEM((R, D), F32),
        lefts=pltpu.VMEM((L, 4, R, D), BF),
        left_t=pltpu.VMEM((L, left_rows(cfg), D), BF),
        sent=pltpu.VMEM((L, cfg.ND, SLOT, wide), BF),
        got=pltpu.VMEM((L, cfg.N, SLOT, wide), BF),
        flat=pltpu.VMEM((L, cfg.HG, rows_t, C3), BF),
        reply=pltpu.VMEM((L, cfg.HG, cfg.N, SLOT, cfg.C), BF),
        back=pltpu.VMEM((L, cfg.HG, cfg.ND, SLOT, cfg.C), BF),
        qkv=pltpu.VMEM((L, R, 3 * D), BF),
        n2=pltpu.VMEM((R, D), BF),
        hidden=pltpu.VMEM((R, cfg.FW), BF),
        full=pltpu.VMEM((L, cfg.T, R, D), BF),
        part=pltpu.VMEM((2, cfg.T, R, D), BF),
        from_mate=pltpu.VMEM((L, 2, R, D), BF),
        from_across=pltpu.VMEM((L, R, D), BF),
        w_sems=pltpu.SemaphoreType.DMA((len(WEIGHTS),)),
        swap_sems=pltpu.SemaphoreType.DMA((2, 2 * cfg.T)),
        key_sems=pltpu.SemaphoreType.DMA((2,)),
        time_sems=pltpu.SemaphoreType.DMA((L, cfg.HG, 4)),
        tp_sems=pltpu.SemaphoreType.DMA((L, 12)),
        save_sems=pltpu.SemaphoreType.DMA((4 + L * (7 + cfg.HG),)),
    )
    def build(*args, **options):
        return pl.pallas_call(*args, **options)

    return call(build, forward_kernel, inputs, outputs, scratch, cid, cfg=cfg)


def reverse(index, bits):
    return sum(((index >> bit) & 1) << (bits - 1 - bit) for bit in range(bits))


def add(a, b):
    return (a.astype(F32) + b.astype(F32)).astype(BF)


class Pipe:
    def __init__(self, stages, partners, credits, total, slots, gaps, held, every):
        self.stages, self.partners, self.credits, self.total, self.every = stages, partners, credits, total, every
        self.slots, self.gaps, self.held = slots, gaps, held
        self.jobs, self.clock = [], 0
        self.done = [[] for _ in stages]
        self.last = len(stages) - 1

    def add_jobs(self, *jobs):
        self.jobs += jobs

    def ready(self, i, k):
        if i == 0:
            if k >= len(self.jobs) or (k >= self.held and len(self.done[1]) <= k - self.held):
                return False
            if k and self.clock - self.done[0][-1] < self.every:
                return False
        elif k >= len(self.done[i - 1]) or self.clock - self.done[i - 1][k] < self.gaps[i]:
            return False
        return i == self.last or k < self.slots or len(self.done[min(i + 2, self.last)]) > k - self.slots

    def tick(self):
        self.clock += 1
        for i in reversed(range(len(self.stages))):
            k = len(self.done[i])
            if not self.ready(i, k):
                continue
            if i < self.last and k >= self.slots:
                for at, _ in self.partners(i):
                    pl.semaphore_wait(self.credits.at[at], 1)
            self.stages[i](k, self.jobs[k])
            self.done[i].append(self.clock)
            if k + self.slots < self.total:
                for sender in range(self.last):
                    if min(sender + 2, self.last) == i:
                        for at, to in self.partners(sender):
                            pl.semaphore_signal(self.credits.at[at], inc=1, device_id=to, device_id_type=MESH)

    @property
    def open(self):
        return len(self.done[-1]) < len(self.jobs)


def attn_pipe(r, cfg):
    S, D, T = cfg.S, cfg.D, cfg.T
    bits = S.bit_length() - 1
    rows, half = D // S, D // 2
    seq, rank = lax.axis_index("seq"), lax.axis_index("tp")
    core, chip = rank % 2, rank // 2
    sends, recvs = r.sum_sends, r.sum_recvs
    held, slots = r.partial.shape[0], r.core_in.shape[0]
    seq_in = [getattr(r, f"seq_in{bit}") for bit in range(bits)]

    def remote(source, target, i, k, **to):
        return pltpu.make_async_remote_copy(
            source, target, sends.at[i, k % slots], recvs.at[i, k % slots], device_id=to, device_id_type=MESH
        )

    def core_copy(k):
        return remote(r.partial.at[k % held, 1 - core], r.core_in.at[k % slots], 0, k, tp=rank ^ 1)

    def x_copy(k):
        return remote(r.core_in.at[k % slots, :, 1 - chip], r.x_in.at[k % slots], 1, k, tp=rank ^ 2)

    def bit_copy(k, bit):
        source = r.x_in if bit == 0 else seq_in[bit - 1]
        size = S >> (bit + 1)
        other = 1 - (seq >> bit) % 2
        return remote(
            source.at[k % slots, pl.ds(other * size, size)], seq_in[bit].at[k % slots], 2 + bit, k, seq=seq ^ (1 << bit)
        )

    def final_copy(k, i):
        ref = r.final.at[k % slots, rank]
        return remote(ref, ref, 1 + bits + i, k, tp=rank ^ i)

    def compute(k, job):
        left, right, _, _ = job
        for side in range(2):
            value = dot(left[...], right[:, side * half : side * half + half], TN).astype(BF)
            for s in range(S):
                r.partial[k % held, side, reverse(s, bits)] = value[s * rows : (s + 1) * rows].reshape(2, rows // 2, half)
        core_copy(k).start()

    def from_core(k, job):
        core_copy(k).wait()
        r.core_in[k % slots] = add(r.core_in[k % slots], r.partial[k % held, core])
        x_copy(k).start()

    def from_x(k, job):
        x_copy(k).wait()
        r.x_in[k % slots] = add(r.x_in[k % slots], r.core_in[k % slots, :, chip])
        bit_copy(k, 0).start()

    def from_bit(k, job, bit):
        bit_copy(k, bit).wait()
        size = S >> (bit + 1)
        before = r.x_in if bit == 0 else seq_in[bit - 1]
        own = before[k % slots, pl.ds(((seq >> bit) % 2) * size, size)]
        value = add(seq_in[bit][k % slots], own)
        if bit < bits - 1:
            seq_in[bit][k % slots] = value
            bit_copy(k, bit + 1).start()
        else:
            r.final[k % slots, rank] = value[0]
            for i in range(1, T):
                final_copy(k, i).start()

    def finish(k, job):
        _, _, layer, columns = job
        for i in range(1, T):
            final_copy(k, i).wait()
        if k >= 2:
            wait_bytes(r.attn_out.at[k % 2], r.out_sems.at[k % 2])
        for q in range(T):
            at = (q // 2) * (rows // 2)
            r.attn_out[k % 2, at : at + rows // 2, (q % 2) * half : (q % 2) * half + half] = r.final[k % slots, q].astype(F32)
        for column, first, size in columns:
            pltpu.make_async_copy(
                r.attn_out.at[k % 2, :, pl.ds(first, size)], r.o_attn.at[layer, :, pl.ds(column, size)], r.out_sems.at[k % 2]
            ).start()

    stages = [compute, from_core, from_x]
    stages += [functools.partial(from_bit, bit=bit) for bit in range(bits)]
    stages += [finish]

    def partners(i):
        if i < 2:
            return [(i, {"tp": rank ^ (1 << i)})]
        if i < 2 + bits:
            return [(i, {"seq": seq ^ (1 << (i - 2))})]
        return [(1 + bits + j, {"tp": rank ^ j}) for j in range(1, T)]

    pipe = Pipe(stages, partners, r.credits, 9 * LAYERS, slots, [0, 1, 8] + [4] * bits + [4], held, 1)

    def flush():
        for k in range(2):
            wait_bytes(r.attn_out.at[k], r.out_sems.at[k])

    return pipe, flush


def fc_pipe(r, cfg):
    S, D, T, R = cfg.S, cfg.D, cfg.T, cfg.R
    bits = S.bit_length() - 1
    rows = D // S
    width = r.fc_part.shape[-1]
    seq = lax.axis_index("seq")
    held, slots = r.fc_part.shape[0], r.fc_in0.shape[0]
    fc_in = [getattr(r, f"fc_in{bit}") for bit in range(bits)]

    def bit_copy(k, bit):
        source = r.fc_part.at[k % held] if bit == 0 else fc_in[bit - 1].at[k % slots]
        size = S >> (bit + 1)
        other = 1 - (seq >> bit) % 2
        return pltpu.make_async_remote_copy(
            source.at[pl.ds(other * size, size)],
            fc_in[bit].at[k % slots],
            r.fc_sends.at[bit, k % slots],
            r.fc_recvs.at[bit, k % slots],
            device_id={"seq": seq ^ (1 << bit)},
            device_id_type=MESH,
        )

    def compute(k, job):
        left, right, (place, column) = job
        value = dot(left[...].reshape(T * R, D), right[:, :, column : column + width].reshape(T * R, width), TN).astype(BF)
        for s in range(S):
            r.fc_part[k % held, reverse(s, bits)] = value[s * rows : (s + 1) * rows]
        bit_copy(k, 0).start()

    def from_bit(k, job, bit):
        _, _, (place, column) = job
        bit_copy(k, bit).wait()
        size = S >> (bit + 1)
        mine = pl.ds(((seq >> bit) % 2) * size, size)
        own = r.fc_part[k % held, mine] if bit == 0 else fc_in[bit - 1][k % slots, mine]
        if bit < bits - 1:
            fc_in[bit][k % slots] = add(fc_in[bit][k % slots], own)
            bit_copy(k, bit + 1).start()
        else:
            r.o_fc[place, :, column : column + width] = own[0].astype(F32) + fc_in[bit][k % slots, 0].astype(F32)

    stages = [compute] + [functools.partial(from_bit, bit=bit) for bit in range(bits)]


    def partners(i):
        return [(i, {"seq": seq ^ (1 << i)})]

    total = 2 * LAYERS * (cfg.FW // width)
    return Pipe(stages, partners, r.fc_credits, total, slots, [0] + [7] * bits, held, 1)


STATE = ["x", "mid", "after", "flat", "qkv", "full"]


def backward_kernel(r, cfg):
    D, R, T = cfg.D, cfg.R, cfg.T
    me = my_index(cfg)
    rows_t = cfg.N * SLOT
    C, C3 = cfg.C, 3 * cfg.C
    blocks = row_blocks(cfg)
    weights = Weights(r)
    state = {}

    def load(layer, *names):
        for name in names:
            copy = pltpu.make_async_copy(getattr(r, "i_" + name).at[layer], getattr(r, name), r.state_sems.at[STATE.index(name)])
            copy.start()
            state[name] = copy

    def get(name):
        if name in state:
            state.pop(name).wait()
        return getattr(r, name)

    top = LAYERS - 1
    load_grad = pltpu.make_async_copy(r.i_grad, r.grad, r.load_sems.at[0])
    load_lefts = pltpu.make_async_copy(r.i_lefts, r.lefts, r.load_sems.at[1])
    load_grad.start()
    load(top, "full")
    weights.load(top, "up", "down")
    load(top, "after")
    weights.load(top, "sproj")
    load(top, "qkv", "mid")
    load_lefts.start()
    load_left_t = pltpu.make_async_copy(r.i_left_t, r.left_t, r.load_sems.at[2])
    load_left_t.start()
    weights.load(top, "sqkv", "tfc", "tproj", "tqkv")
    load(top, "flat", "x")
    greet_all(cfg, me)
    out_swap = swap_tp(r.i_last, r.o_out, r.swap_sems.at[0])
    attn, flush = attn_pipe(r, cfg)
    fc = fc_pipe(r, cfg)
    loaded = []

    def beside(count):
        for _ in range(count):
            fc.tick()
            attn.tick()

    load_grad.wait()
    grad = r.grad
    for layer in reversed(range(LAYERS)):
        ends = []
        att, proj, n1, so = (r.lefts.at[layer, i] for i in range(4))
        dqkv_t, dqkv_s = r.dqkv_t.at[layer], r.dqkv_s.at[layer]
        gt1, gt2, gu = (r.rights.at[layer, i] for i in range(3))
        sems = r.tp_sems.at[layer]

        r.gm[...] = grad[...].astype(BF)
        full, up, down = get("full"), weights.get("up"), weights.get("down")

        def work(q, full=full, up=up, down=down):
            rows, back = full[q], r.full_grad[q]
            for first in range(0, cfg.FW, 256):
                columns = slice(first, min(first + 256, cfg.FW))
                value = dot(rows, up[:, columns])
                cdf = 0.5 * (1.0 + lax.erf(value * 0.7071067811865476))
                slope = cdf + value * jnp.exp(-0.5 * value * value) * 0.3989422804014327
                r.hidden[q, :, columns] = (value * cdf).astype(BF)
                r.grad_pre[q, :, columns] = (slope * dot(back, down[columns, :], NT)).astype(BF)
            r.part[q] = dot(r.grad_pre[q], up[...], NT).astype(BF)

        ends += [copy.wait_send for copy in gather_tp(r.gm, r.full_grad, sems.at[pl.ds(0, 6)], work, lambda: beside(1))]

        def weights_part(layer=layer):
            width = r.fc_part.shape[-1]
            for column in range(0, cfg.FW, width):
                fc.add_jobs((r.full, r.grad_pre, (layer, column)), (r.full_grad, r.hidden, (LAYERS + layer, column)))
            beside(4)

        def write(rows, value):
            r.delta[rows, :] = value

        ends += [
            copy.wait_send
            for copy in scatter_tp(r.part, r.from_mate, r.from_across, sems.at[pl.ds(6, 6)], weights_part, write, blocks)
        ]
        for wait in ends:
            wait()
        ends.clear()
        after = get("after")
        norm_backward(cfg, after, r.gain[layer, 2:3, :], lambda rows: r.delta[rows, :], grad, r.sums, layer, 2)
        gu[...] = grad[...].astype(BF)
        if not loaded:
            load_lefts.wait()
            load_left_t.wait()
            loaded.append(1)
        attn.add_jobs((so, gu, layer, [(8 * D, 0, D)]))
        beside(1)

        r.gso[...] = dot(gu[...], weights.get("sproj")[...], NT).astype(BF)
        beside(1)

        def write(first, rows, part, pair, value, dqkv_s=dqkv_s):
            start = part * D + pair * 128
            dqkv_s[pl.ds(first, rows), start : start + 128] = value.astype(BF)

        for pair in range(D // 128):
            attend_back(get("qkv"), r.gso, r.space_col, r.space_row, write, r.acc, [pair])
            beside(1)
        attn.add_jobs(*[(n1, dqkv_s.at[:, pl.ds(i * D, D)], layer, [((5 + i) * D, 0, D)]) for i in range(3)])
        sqkv = weights.get("sqkv")
        r.delta[...] = sum(dot(dqkv_s[:, i * D : i * D + D], sqkv[:, i * D : i * D + D], NT) for i in range(3))
        beside(1)
        norm_backward(cfg, get("mid"), r.gain[layer, 1:2, :], lambda rows: r.delta[rows, :], grad, r.sums, layer, 1)
        beside(1)

        for rows in blocks:
            gt2[rows, :] = jnp.where(patch_rows(cfg, rows), grad[rows, :], 0.0).astype(BF)
        gt1[...] = dot(gt2[...], weights.get("tfc")[...], NT).astype(BF)
        attn.add_jobs((proj, gt2, layer, [(4 * D, 0, D)]), (att, gt1, layer, [(3 * D, 0, D)]))
        beside(1)
        tproj = weights.get("tproj")
        sems = r.time_sems.at[layer]
        for group in range(cfg.HG):
            for split in range(cfg.HS):
                first = head_columns(cfg, split, group)
                value = dot(gt1[...], tproj[first : first + C, :], NT).astype(BF)
                r.sent[group, split * cfg.G : (split + 1) * cfg.G] = value.reshape(cfg.G, SLOT, C)
            spread(cfg, me, r.sent.at[group], r.got.at[group], sems.at[group, 0], sems.at[group, 1])
            ends.append(functools.partial(spread_sent, cfg, me, r.sent.at[group], sems.at[group, 0]))
            beside(1)
        flat, tqkv = get("flat"), weights.get("tqkv")
        for group in range(cfg.HG):

            def write(first, rows, part, pair, value, group=group, dqkv_t=dqkv_t):
                start = part * C + pair * 128
                if cfg.HS == 1:
                    start += group * C3
                    dqkv_t[pl.ds(first, rows), start : start + 128] = value.astype(BF)
                else:
                    chunks = pl.ds(first // SLOT, rows // SLOT)
                    r.reply[0, chunks, :, start : start + 128] = value.astype(BF).reshape(rows // SLOT, SLOT, 128)

            for pair in range(C // 128):

                @pl.when(me < cfg.ND)
                def _(group=group, sems=sems, pair=pair, write=write):
                    if pair == 0:
                        wait_bytes(r.got.at[group], sems.at[group, 1])
                        r.flat_grad[...] = r.got[group].reshape(rows_t, C)
                    attend_back(flat.at[group], r.flat_grad, r.kcol, r.krow, write, r.acc, [pair])

                beside(1)
            if cfg.HS == 1:

                @pl.when(me >= cfg.ND)
                def _(group=group, dqkv_t=dqkv_t):
                    dqkv_t[:, group * C3 : (group + 1) * C3] = jnp.zeros((rows_t, C3), BF)

                columns = [(part * D + group * C, part * C, C) for part in range(3)]
                attn.add_jobs((r.left_t.at[layer], dqkv_t.at[:, pl.ds(group * C3, C3)], layer, columns))

        for group in range(cfg.HG):

            @pl.when(me < cfg.ND)
            def _(group=group, sems=sems, dqkv_t=dqkv_t, tqkv=tqkv):
                if cfg.HS == 1:
                    rows = slice(group * C, (group + 1) * C)
                    value = sum(
                        dot(dqkv_t[:, g * C3 + i * C : g * C3 + (i + 1) * C], tqkv[rows, i * D + g * C : i * D + (g + 1) * C], NT)
                        for g in range(cfg.HG)
                        for i in range(3)
                    )
                    r.reply[group] = value.astype(BF).reshape(cfg.N, SLOT, C)
                collect(cfg, me, r.reply.at[group], r.back.at[group], sems.at[group, 2], sems.at[group, 3])

            ends.append(functools.partial(collect_sent, cfg, me, r.reply.at[group], sems.at[group, 2]))
            beside(1)
        if cfg.HS == 1:
            for group in range(cfg.HG):
                beside(1)
                wait_bytes(r.back.at[group], sems.at[group, 3])
                r.delta[:, group * C : (group + 1) * C] = r.back[group].reshape(R, C).astype(F32)
        else:
            wait_bytes(r.back.at[0], sems.at[0, 3])
            for split in range(cfg.HS):
                first = head_columns(cfg, split, 0)
                for part in range(3):
                    value = r.back[0, split * cfg.G : (split + 1) * cfg.G, :, part * C : (part + 1) * C]
                    dqkv_t[:, part * D + first : part * D + first + C] = value.reshape(R, C)
            attn.add_jobs(
                *[(r.left_t.at[layer], dqkv_t.at[:, pl.ds(i * D, D)], layer, [(i * D, 0, D)]) for i in range(3)]
            )
            r.delta[...] = sum(dot(dqkv_t[:, i * D : i * D + D], tqkv[:, i * D : i * D + D], NT) for i in range(3))
        beside(1)
        norm_backward(cfg, get("x"), r.gain[layer, 0:1, :], lambda rows: r.delta[rows, :], grad, r.sums, layer, 0)
        while len(fc.done[0]) < len(fc.jobs):
            beside(1)
        for wait in ends:
            wait()
        if layer:
            load(layer - 1, *STATE)
            weights.load(layer - 1, *WEIGHTS)

    rest = r.sums.shape[0] - 6 * LAYERS
    if rest:
        r.sums[6 * LAYERS :, :] = jnp.zeros((rest, D), F32)

    def window(seq):
        return pl.ds(pl.multiple_of(norm_window(cfg, seq), 128), r.norm_in.shape[2])

    def norm_copy(to):
        return send_copy(
            cfg, r.sums.at[:, window(to // T)], r.norm_in.at[me], r.norm_sems.at[0], r.norm_sems.at[1], to
        )

    to_all(cfg, me, norm_copy)
    pltpu.make_async_copy(r.sums.at[:, window(lax.axis_index("seq"))], r.norm_in.at[me], r.norm_sems.at[1]).start()
    own_rows = R // T
    for q in range(T):
        r.grad_out[q] = grad[q * own_rows : (q + 1) * own_rows, :].astype(BF)
    r.o_cls[...] = grad[SLOT - 1 : SLOT, :]
    grad_swap = swap_tp(r.grad_out, r.o_grad, r.swap_sems.at[1])
    while attn.open or fc.open:
        beside(1)
    flush()
    wait_bytes(r.norm_in, r.norm_sems.at[1])
    r.o_norm[...] = jnp.sum(r.norm_in[...], 0)
    wait_bytes(r.norm_in.at[pl.ds(0, cfg.N - 1)], r.norm_sems.at[0])
    for copy in out_swap + grad_swap:
        copy.wait()


def norm_window(cfg, seq):
    return jnp.minimum((seq * (cfg.D // cfg.S)) // 128 * 128, cfg.D - 256)


def backward(cfg, arrays, kept, cid):
    D, R, T, L, S, FW = cfg.D, cfg.R, cfg.T, LAYERS, cfg.S, cfg.FW
    rows_t, C, C3 = cfg.N * SLOT, cfg.C, 3 * cfg.C
    own_rows = R // T
    bits = S.bit_length() - 1
    rows, half = D // S, D // 2
    small = (rows // 2, half)
    width = FW // 2
    held, slots, fc_held, fc_slots = (3, 6, 3, 4) if small[0] % 16 == 0 else (1, 2, 1, 2)
    inputs = dict(
        gain=(arrays["gain"], VM),
        kcol=(kept["o_kcol"], VM),
        krow=(kept["o_krow"], VM),
        space_col=(arrays["space_col"], VM),
        space_row=(arrays["space_row"], VM),
        i_last=(kept["last"], ANY),
        i_grad=(kept["o_grad"], ANY),
        i_lefts=(kept["o_lefts"], ANY),
        i_left_t=(kept["o_left_t"], ANY),
    )
    inputs |= {"i_" + name: (kept["o_" + name], ANY) for name in STATE}
    inputs |= {"w_" + name: (arrays["w_" + name], ANY) for name in WEIGHTS}
    outputs = dict(
        o_out=((T, own_rows, D), BF, ANY),
        o_grad=((T, own_rows, D), BF, ANY),
        o_cls=((1, D), F32, VM),
        o_attn=((L, rows, 9 * D), F32, ANY),
        o_fc=((2 * L, rows, FW), F32, VM),
        o_norm=((6 * L + -6 * L % 8, 256), F32, VM),
    )
    scratch = weight_scratch(cfg) | dict(
        x=pltpu.VMEM((R, D), F32),
        mid=pltpu.VMEM((R, D), F32),
        after=pltpu.VMEM((R, D), F32),
        flat=pltpu.VMEM((cfg.HG, rows_t, C3), BF),
        qkv=pltpu.VMEM((R, 3 * D), BF),
        full=pltpu.VMEM((T, R, D), BF),
        grad=pltpu.VMEM((R, D), F32),
        delta=pltpu.VMEM((R, D), F32),
        lefts=pltpu.VMEM((L, 4, R, D), BF),
        left_t=pltpu.VMEM((L, left_rows(cfg), D), BF),
        rights=pltpu.VMEM((L, 3, R, D), BF),
        dqkv_t=pltpu.VMEM((L, left_rows(cfg), 3 * D), BF),
        dqkv_s=pltpu.VMEM((L, R, 3 * D), BF),
        gm=pltpu.VMEM((R, D), BF),
        gso=pltpu.VMEM((R, D), BF),
        full_grad=pltpu.VMEM((T, R, D), BF),
        hidden=pltpu.VMEM((T, R, FW), BF),
        grad_pre=pltpu.VMEM((T, R, FW), BF),
        part=pltpu.VMEM((T, R, D), BF),
        from_mate=pltpu.VMEM((2, R, D), BF),
        from_across=pltpu.VMEM((R, D), BF),
        sent=pltpu.VMEM((cfg.HG, cfg.ND, SLOT, C), BF),
        got=pltpu.VMEM((cfg.HG, cfg.N, SLOT, C), BF),
        flat_grad=pltpu.VMEM((rows_t, C), BF),
        reply=pltpu.VMEM((cfg.HG, cfg.N, SLOT, C if cfg.HS == 1 else C3), BF),
        back=pltpu.VMEM((cfg.HG, cfg.ND, SLOT, C if cfg.HS == 1 else C3), BF),
        acc=pltpu.VMEM((2, rows_t if rows_t > 256 else 8, 128), F32),
        sums=pltpu.VMEM((6 * L + -6 * L % 8, D), F32),
        norm_in=pltpu.VMEM((cfg.N, 6 * L + -6 * L % 8, 256), F32),
        grad_out=pltpu.VMEM((T, own_rows, D), BF),
        partial=pltpu.VMEM((held, 2, S, 2) + small, BF),
        core_in=pltpu.VMEM((slots, S, 2) + small, BF),
        x_in=pltpu.VMEM((slots, S) + small, BF),
        final=pltpu.VMEM((slots, T) + small, BF),
        attn_out=pltpu.VMEM((2, rows, D), F32),
        fc_part=pltpu.VMEM((fc_held, S, rows, width), BF),
        w_sems=pltpu.SemaphoreType.DMA((len(WEIGHTS),)),
        state_sems=pltpu.SemaphoreType.DMA((len(STATE),)),
        load_sems=pltpu.SemaphoreType.DMA((3,)),
        swap_sems=pltpu.SemaphoreType.DMA((2, 2 * T)),
        time_sems=pltpu.SemaphoreType.DMA((L, cfg.HG, 4)),
        tp_sems=pltpu.SemaphoreType.DMA((L, 12)),
        sum_sends=pltpu.SemaphoreType.DMA((1 + bits + T, slots)),
        sum_recvs=pltpu.SemaphoreType.DMA((1 + bits + T, slots)),
        fc_sends=pltpu.SemaphoreType.DMA((bits, fc_slots)),
        fc_recvs=pltpu.SemaphoreType.DMA((bits, fc_slots)),
        out_sems=pltpu.SemaphoreType.DMA((2,)),
        norm_sems=pltpu.SemaphoreType.DMA((2,)),
        credits=pltpu.SemaphoreType.REGULAR((1 + bits + T,)),
        fc_credits=pltpu.SemaphoreType.REGULAR((bits,)),
    )
    for bit in range(bits):
        scratch[f"seq_in{bit}"] = pltpu.VMEM((slots, S >> (bit + 1)) + small, BF)
        scratch[f"fc_in{bit}"] = pltpu.VMEM((fc_slots, S >> (bit + 1), rows, width), BF)
    def build(*args, **options):
        return pl.pallas_call(*args, **options)

    return call(build, backward_kernel, inputs, outputs, scratch, cid, cfg=cfg)


def shards(
    cfg,
    patches,
    cls_tokens,
    frame_clip,
    norm_gain,
    norm_bias,
    w_tqkv,
    w_tproj,
    w_tfc,
    w_sqkv,
    w_sproj,
    w_fc1,
    w_fc2,
    cot_patches,
    cot_cls,
):
    frames, local, D = patches.shape
    groups = local // cfg.PER
    slot = jnp.arange(SLOT)
    own_clip = lax.dynamic_index_in_dim(frame_clip, lax.axis_index("tp"), 0, keepdims=False)
    key = jnp.broadcast_to((own_clip * SLOT + slot)[:, None].astype(F32), (SLOT, 128))
    row = jnp.arange(cfg.R)
    space_row = jnp.where((row % SLOT < cfg.PER) | (row == SLOT - 1), 0.0, 1.0).astype(F32)[None, :]

    def padded(x):
        x = x.reshape(frames, groups, cfg.PER, D)
        return jnp.pad(x, ((0, 0), (0, 0), (0, SLOT - cfg.PER), (0, 0))).reshape(frames, groups * SLOT, D)

    arrays = dict(
        patches=padded(patches),
        cots=padded(cot_patches),
        key=key,
        cls=cls_tokens,
        cot_cls=cot_cls,
        gain=norm_gain,
        bias=norm_bias,
        space_col=jnp.zeros((cfg.R, 1), F32),
        space_row=space_row,
        w_tqkv=w_tqkv,
        w_tproj=w_tproj,
        w_tfc=w_tfc,
        w_sqkv=w_sqkv,
        w_sproj=w_sproj,
        w_up=w_fc1,
        w_down=w_fc2,
    )
    kept = forward(cfg, arrays, 0)
    last = kept["o_last"].astype(BF)
    kept["last"] = last.reshape(cfg.T, -1, D)
    out = backward(cfg, arrays, kept, 1)

    def unpadded(x):
        return x.reshape(frames, groups, SLOT, D)[:, :, : cfg.PER].reshape(frames, local, D)

    rows = D // cfg.S
    seq = lax.axis_index("seq")
    norm = lax.dynamic_slice_in_dim(out["o_norm"][: 6 * LAYERS], seq * rows - norm_window(cfg, seq), rows, 1)
    fc = out["o_fc"]
    return (
        unpadded(out["o_out"]),
        last[SLOT - 1 : SLOT],
        unpadded(out["o_grad"]).astype(F32),
        out["o_cls"],
        out["o_attn"],
        norm.reshape(LAYERS, 6, rows),
        fc[:LAYERS],
        jnp.swapaxes(fc[LAYERS:], 1, 2),
    )


def solution(mesh):
    S, T = mesh.shape["seq"], mesh.shape["tp"]

    def run(*args):
        local, D, FW = args[0].shape[1] // T, args[0].shape[2], args[10].shape[2] // T
        per = max(n for n in range(1, SLOT) if local % n == 0)
        groups = args[0].shape[1] // per
        pairs = D // (2 * HEAD_DIM)
        splits = max(n for n in range(1, pairs + 1) if pairs % n == 0 and (n == 1 or groups * n <= S * T))
        head_groups = 3 if splits == 1 and pairs % 3 == 0 else 1
        cfg = Cfg(
            S, T, S * T, D, groups, groups * SLOT, per, splits, groups * splits, head_groups, D // (splits * head_groups), FW
        )
        return jax.shard_map(
            functools.partial(shards, cfg),
            mesh=mesh,
            in_specs=(
                P("seq", "tp", None),
                P(("seq", "tp"), None),
                P("seq"),
                P(),
                P(),
                P(),
                P(),
                P(),
                P(),
                P(),
                P(None, None, "tp"),
                P(None, "tp", None),
                P("seq", "tp", None),
                P(("seq", "tp"), None),
            ),
            out_specs=(
                P("seq", "tp", None),
                P(("seq", "tp"), None),
                P("seq", "tp", None),
                P(("seq", "tp"), None),
                P(None, "seq", None),
                P(None, None, "seq"),
                P(None, "seq", "tp"),
                P(None, "tp", "seq"),
            ),
            check_vma=False,
        )(*args)

    return run
```

```python
import functools
from collections import namedtuple
from types import SimpleNamespace

import jax
import jax.numpy as jnp
from jax import lax
from jax.experimental import pallas as pl
from jax.experimental.pallas import tpu as pltpu
from jax.sharding import PartitionSpec as P

HEAD_DIM = 64
LAYERS = 2
SLOT = 8
EPS = 1e-06
NEG_FILL = -1e30
MESH = pl.DeviceIdType.MESH
BF = jnp.bfloat16
F32 = jnp.float32
NN = (((1,), (0,)), ((), ()))
NT = (((1,), (1,)), ((), ()))
TN = (((0,), (0,)), ((), ()))
VMEM_LIMIT = 62 * 1024 * 1024
BLOCK = 32

Cfg = namedtuple("Cfg", ["S", "T", "N", "D", "G", "R", "PER", "HS", "ND", "HG", "C", "FW"])


def dot(left, right, dims=NN):
    return lax.dot_general(left, right, dims, preferred_element_type=F32)


def params(cid=None):
    return pltpu.CompilerParams(
        collective_id=cid, has_side_effects=cid is not None, vmem_limit_bytes=VMEM_LIMIT
    )


ANY = pl.BlockSpec(memory_space=pl.ANY)
VM = pl.BlockSpec(memory_space=pltpu.VMEM)


def my_index(cfg):
    return lax.axis_index("seq") * cfg.T + lax.axis_index("tp")


def device(cfg, index):
    return (index // cfg.T, lax.rem(index, cfg.T))


def greet_all(cfg, me):
    barrier = pltpu.get_barrier_semaphore()

    def signal(i, carry):
        pl.semaphore_signal(
            barrier, inc=1, device_id=device(cfg, lax.rem(me + i, cfg.N)), device_id_type=MESH
        )
        return carry

    lax.fori_loop(1, cfg.N, signal, 0)
    pl.semaphore_wait(barrier, cfg.N - 1)


def wait_bytes(ref, sem):
    pltpu.make_async_copy(ref, ref, sem).wait()


def head_pair(ref, rows, width, part, pair):
    start = part * width + pair * 128
    return ref[rows, start : start + 128]


def softmax_rows(query, key, mask):
    scores = jnp.where(mask, dot(query, key, NT), NEG_FILL)
    top = jnp.max(scores, -1, keepdims=True)
    weight = jnp.exp(scores - top)
    return weight * (1.0 / jnp.sum(weight, -1, keepdims=True))


def for_row_blocks(total, step, block):
    if total == step:
        block(0)
    else:

        def body(i, carry):
            block(pl.multiple_of(i * step, step))
            return carry

        lax.fori_loop(0, total // step, body, 0)


def attend(qkv, kcol, krow, write):
    total, width = qkv.shape[0], qkv.shape[1] // 3
    step = total if total <= 256 else 64
    every = slice(0, total)
    lane = lax.broadcasted_iota(jnp.int32, (step, 128), 1) < HEAD_DIM
    zero = jnp.zeros((), BF)

    def block(first):
        rows = pl.ds(first, step)
        mask = kcol[rows, :] == krow[...]
        for pair in range(width // 128):
            query = head_pair(qkv, rows, width, 0, pair) * jnp.asarray(HEAD_DIM**-0.5, BF)
            key = head_pair(qkv, every, width, 1, pair)
            value = head_pair(qkv, every, width, 2, pair)
            prob0 = softmax_rows(jnp.where(lane, query, zero), key, mask).astype(BF)
            prob1 = softmax_rows(jnp.where(lane, zero, query), key, mask).astype(BF)
            write(first, step, pair, jnp.where(lane, dot(prob0, value), dot(prob1, value)))

    for_row_blocks(total, step, block)


def attend_back(qkv, grad, kcol, krow, write, acc, pairs):
    total, width = qkv.shape[0], qkv.shape[1] // 3
    step = total if total <= 256 else 64
    every = slice(0, total)
    lane = lax.broadcasted_iota(jnp.int32, (step, 128), 1) < HEAD_DIM
    lane_all = lax.broadcasted_iota(jnp.int32, (total, 128), 1) < HEAD_DIM
    zero = jnp.zeros((), BF)
    scale = HEAD_DIM**-0.5

    for pair in pairs:

        def block(first, pair=pair):
            rows = pl.ds(first, step)
            mask = kcol[rows, :] == krow[...]
            key = head_pair(qkv, every, width, 1, pair)
            value = head_pair(qkv, every, width, 2, pair)
            query = head_pair(qkv, rows, width, 0, pair) * jnp.asarray(scale, BF)
            out = grad[rows, pair * 128 : pair * 128 + 128]
            dq, dk, dv = [], [], []
            for lower in (True, False):
                own = (lambda v: jnp.where(lane, v, zero)) if lower else (lambda v: jnp.where(lane, zero, v))
                prob = softmax_rows(own(query), key, mask)
                back = dot(own(out), value, NT)
                delta = jnp.sum(prob * back, -1, keepdims=True)
                score = (prob * (back - delta)).astype(BF)
                dq.append(dot(score, key))
                dk.append(dot(score, query, TN))
                dv.append(dot(prob.astype(BF), out, TN))
            write(first, step, 0, pair, jnp.where(lane, dq[0], dq[1]) * scale)
            grad_key, grad_value = jnp.where(lane_all, dk[0], dk[1]), jnp.where(lane_all, dv[0], dv[1])
            if total == step:
                write(0, total, 1, pair, grad_key)
                write(0, total, 2, pair, grad_value)
            else:
                acc[0] += grad_key
                acc[1] += grad_value

        if total > step:
            acc[...] = jnp.zeros(acc.shape, F32)
        for_row_blocks(total, step, block)
        if total > step:
            write(0, total, 1, pair, acc[0])
            write(0, total, 2, pair, acc[1])


def refs_by_name(names, refs):
    return SimpleNamespace(**dict(zip(names, refs, strict=True)))


def call(build, kernel, inputs, outputs, scratch, cid, **fixed):
    def body(*refs):
        kernel(refs_by_name([*inputs, *outputs, *scratch], refs), **fixed)

    results = build(
        body,
        out_shape=[jax.ShapeDtypeStruct(shape, dtype) for shape, dtype, _ in outputs.values()],
        in_specs=[spec for _, spec in inputs.values()],
        out_specs=[spec for _, _, spec in outputs.values()],
        scratch_shapes=list(scratch.values()),
        compiler_params=params(cid),
    )(*[array for array, _ in inputs.values()])
    return dict(zip(outputs, results, strict=True))


def row_blocks(cfg):
    return [slice(first, min(first + BLOCK, cfg.R)) for first in range(0, cfg.R, BLOCK)]


def normalize(x):
    center = x - jnp.mean(x, -1, keepdims=True)
    root = lax.rsqrt(jnp.mean(center * center, -1, keepdims=True) + EPS)
    return center * root, root


def norm_forward(cfg, src, gain, bias, out):
    for rows in row_blocks(cfg):
        value = (normalize(src[rows, :])[0] * gain + bias).astype(BF)
        if len(out.shape) == 2:
            out[rows, :] = value
        else:
            chunks = slice(rows.start // SLOT, rows.stop // SLOT)
            out[chunks] = value.reshape(chunks.stop - chunks.start, SLOT, cfg.D)


def norm_backward(cfg, src, gain, grad_of, total, sums, layer, which):
    by_gain = by_bias = None
    for rows in row_blocks(cfg):
        normal, root = normalize(src[rows, :])
        grad = grad_of(rows)
        scaled = grad * gain
        inner = jnp.mean(scaled * normal, -1, keepdims=True)
        total[rows, :] += root * (scaled - jnp.mean(scaled, -1, keepdims=True) - normal * inner)
        eights = (grad.shape[0] // 8, 8, grad.shape[1])
        one, two = jnp.sum((grad * normal).reshape(eights), 0), jnp.sum(grad.reshape(eights), 0)
        by_gain = one if by_gain is None else by_gain + one
        by_bias = two if by_bias is None else by_bias + two
    at = layer * 6 + which
    sums[at : at + 1, :] = jnp.sum(by_gain, 0, keepdims=True)
    sums[at + 3 : at + 4, :] = jnp.sum(by_bias, 0, keepdims=True)


def space_keys(cfg):
    row = lax.broadcasted_iota(jnp.int32, (1, cfg.R), 1)
    used = (lax.rem(row, SLOT) < cfg.PER) | (row == SLOT - 1)
    return jnp.zeros((cfg.R, 1), F32), jnp.where(used, 0.0, 1.0)


def patch_rows(cfg, rows):
    row = lax.broadcasted_iota(jnp.int32, (rows.stop - rows.start, 1), 0) + rows.start
    return lax.rem(row, SLOT) < cfg.PER


def to_all(cfg, me, copy_to, only=None):
    def send(i, carry):
        to = me ^ (cfg.N - i)
        if only is None:
            copy_to(to).start()
        else:

            @pl.when(to < only)
            def _():
                copy_to(to).start()

        return carry

    lax.fori_loop(1, cfg.N, send, 0)


def send_copy(cfg, src, dst, send, recv, to):
    return pltpu.make_async_remote_copy(src, dst, send, recv, device_id=device(cfg, to), device_id_type=MESH)


def tp_copy(src, dst, send, recv, rank):
    return pltpu.make_async_remote_copy(src, dst, send, recv, device_id={"tp": rank}, device_id_type=MESH)


def spread(cfg, me, src, dst, send, recv):
    to_all(cfg, me, lambda to: send_copy(cfg, src.at[to], dst.at[me], send, recv, to), cfg.ND)

    @pl.when(me < cfg.ND)
    def _():
        pltpu.make_async_copy(src.at[me], dst.at[me], recv).start()


def spread_sent(cfg, me, src, send):
    @pl.when(me < cfg.ND)
    def _():
        wait_bytes(src.at[pl.ds(0, cfg.ND - 1)], send)

    @pl.when(me >= cfg.ND)
    def _():
        wait_bytes(src, send)


def collect(cfg, me, src, dst, send, recv):
    to_all(cfg, me, lambda to: send_copy(cfg, src.at[to], dst.at[me], send, recv, to))
    pltpu.make_async_copy(src.at[me], dst.at[me], recv).start()


def collect_sent(cfg, me, src, send):
    @pl.when(me < cfg.ND)
    def _():
        wait_bytes(src.at[pl.ds(0, cfg.N - 1)], send)


def left_rows(cfg):
    return cfg.N * SLOT if cfg.HS == 1 else cfg.R


def head_columns(cfg, split, group):
    return (split * cfg.HG + group) * cfg.C


def swap_tp(x, out, sems):
    rank = lax.axis_index("tp")
    ranks = x.shape[0]
    local = pltpu.make_async_copy(x.at[rank], out.at[rank], sems.at[0])
    copies = [
        tp_copy(x.at[rank ^ i], out.at[rank], sems.at[i], sems.at[ranks + i], rank ^ i) for i in range(1, ranks)
    ]
    local.start()
    for copy in copies:
        copy.start()
    return [local, *copies]


def gelu(value):
    return 0.5 * value * (1.0 + lax.erf(value * 0.7071067811865476))


def gelu_slope(value):
    return 0.5 * (1.0 + lax.erf(value * 0.7071067811865476)) + value * jnp.exp(-0.5 * value * value) * 0.3989422804014327


def exchange_tp(cfg, own, full, part, from_mate, from_across, sems, work, beside, last, write):
    rank = lax.axis_index("tp")
    mate, across, far = rank ^ 1, rank ^ 2, rank ^ 3
    size = cfg.R // 2
    halves = [slice(0, size), slice(size, cfg.R)]

    def copies(h, rows):
        at = sems.at[h]
        return SimpleNamespace(
            across=tp_copy(own.at[rows], full.at[rank, rows], at.at[0], at.at[1], across),
            mate=tp_copy(own.at[rows], full.at[rank, rows], at.at[2], at.at[3], mate),
            forward=tp_copy(full.at[across, rows], full.at[across, rows], at.at[4], at.at[5], mate),
            first=tp_copy(part.at[far, rows], from_mate.at[0, rows], at.at[6], at.at[7], mate),
            second=tp_copy(part.at[mate, rows], from_mate.at[1, rows], at.at[8], at.at[9], mate),
            third=tp_copy(part.at[across, rows], from_across.at[rows], at.at[10], at.at[11], across),
        )

    both = [copies(h, rows) for h, rows in enumerate(halves)]
    for half in both:
        half.across.start()
        half.mate.start()
    full[rank] = own[...]
    for half, rows in zip(both, halves, strict=True):
        work(rank, rows)
        half.mate.wait_recv()
        work(mate, rows)
        beside()
    for half, rows in zip(both, halves, strict=True):
        half.across.wait_recv()
        half.forward.start()
        work(across, rows)
        half.forward.wait_recv()
        work(far, rows)
        half.first.start()
        half.second.start()
        beside()
        half.first.wait_recv()
        part[across, rows, :] = (part[across, rows, :].astype(F32) + from_mate[0, rows, :].astype(F32)).astype(BF)
        half.third.start()
    last()
    for half, rows in zip(both, halves, strict=True):
        half.second.wait_recv()
        half.third.wait_recv()
        near = part[rank, rows, :].astype(F32) + from_mate[1, rows, :].astype(F32)
        write(rows, near + from_across[rows, :].astype(F32))
    return [copy.wait_send for half in both for copy in vars(half).values()]


WEIGHTS = ["tqkv", "tproj", "tfc", "sqkv", "sproj", "up", "down"]


def weight_scratch(cfg):
    D, FW = cfg.D, cfg.FW
    shapes = [(D, 3 * D), (D, D), (D, D), (D, 3 * D), (D, D), (D, FW), (FW, D)]
    return {name: pltpu.VMEM(shape, BF) for name, shape in zip(WEIGHTS, shapes, strict=True)}


class Weights:
    def __init__(self, r):
        self.r, self.open = r, {}

    def load(self, layer, *names):
        for name in names:
            at = WEIGHTS.index(name)
            copy = pltpu.make_async_copy(getattr(self.r, "w_" + name).at[layer], getattr(self.r, name), self.r.w_sems.at[at])
            copy.start()
            self.open[name] = copy

    def get(self, name):
        if name in self.open:
            self.open.pop(name).wait()
        return getattr(self.r, name)


def forward_kernel(r, cfg):
    me = my_index(cfg)
    rank = lax.axis_index("tp")
    rows_t = cfg.N * SLOT
    C3 = 3 * cfg.C
    blocks = row_blocks(cfg)
    weights = Weights(r)
    weights.load(0, *WEIGHTS)
    greet_all(cfg, me)
    slot = lax.broadcasted_iota(jnp.int32, r.key.shape, 0)
    r.key[...] = (r.clip[rank] * SLOT + slot).astype(F32)
    r.space_col[...], r.space_row[...] = space_keys(cfg)
    swaps = swap_tp(r.patches, r.patch_in, r.swap_sems.at[0])
    swaps_cot = swap_tp(r.cots, r.cot_in, r.swap_sems.at[1])
    to_all(cfg, me, lambda to: send_copy(cfg, r.key, r.keys.at[me], r.key_sems.at[0], r.key_sems.at[1], to))
    pltpu.make_async_copy(r.key, r.keys.at[me], r.key_sems.at[1]).start()
    ends = []
    saves = []

    def save(src, dst):
        copy = pltpu.make_async_copy(src, dst, r.save_sems.at[len(saves)])
        copy.start()
        saves.append(copy)

    for copy in swaps:
        copy.wait()
    own_rows = cfg.R // cfg.T
    for q in range(cfg.T):
        r.x[0, q * own_rows : (q + 1) * own_rows, :] = r.patch_in[q].astype(F32)
    r.x[0, SLOT - 1 : SLOT, :] = r.cls[...].astype(F32)

    for layer in range(LAYERS):
        x, mid, after = r.x.at[layer], r.mid.at[layer], r.after.at[layer]
        att, proj, n1, so = (r.lefts.at[layer, i] for i in range(4))
        left_t = r.left_t.at[layer]
        save(x, r.o_x.at[layer])
        sems = r.time_sems.at[layer]
        gain0, bias0 = r.norms[0, layer, 0:1, :], r.norms[1, layer, 0:1, :]
        if cfg.HS == 1:
            sent = r.sent.at[layer]
            norm_forward(cfg, x, gain0, bias0, sent)
            spread(cfg, me, sent, r.got.at[layer], sems.at[0, 0], sems.at[0, 1])
            ends.append(functools.partial(spread_sent, cfg, me, sent, sems.at[0, 0]))
        else:
            norm_forward(cfg, x, gain0, bias0, left_t)
            tqkv = weights.get("tqkv")
            sent = r.sent.at[layer]
            for split in range(cfg.HS):
                first = head_columns(cfg, split, 0)
                for part in range(3):
                    value = dot(left_t[...], tqkv[:, part * cfg.D + first : part * cfg.D + first + cfg.C]).astype(BF)
                    sent[split * cfg.G : (split + 1) * cfg.G, :, part * cfg.C : (part + 1) * cfg.C] = value.reshape(
                        cfg.G, SLOT, cfg.C
                    )
            spread(cfg, me, sent, r.got.at[layer], sems.at[0, 0], sems.at[0, 1])
            ends.append(functools.partial(spread_sent, cfg, me, sent, sems.at[0, 0]))

        if layer == 0:
            wait_bytes(r.keys, r.key_sems.at[1])
            keys = r.keys[...].reshape(rows_t, 128)
            r.kcol[...] = keys[:, 0:1]
            r.krow[...] = jnp.transpose(keys)[0:1, :]
            save(r.kcol, r.o_kcol)
            save(r.krow, r.o_krow)

        tqkv = weights.get("tqkv")

        @pl.when(me < cfg.ND)
        def _(layer=layer, sems=sems, tqkv=tqkv, left_t=left_t):
            wait_bytes(r.got.at[layer], sems.at[0, 1])
            if cfg.HS == 1:
                left_t[...] = r.got[layer].reshape(rows_t, cfg.D)
            else:
                r.flat[layer, 0] = r.got[layer].reshape(rows_t, C3)
            for group in range(cfg.HG):
                flat = r.flat.at[layer, group]
                if cfg.HS == 1:
                    for part in range(3):
                        first = part * cfg.D + group * cfg.C
                        value = dot(left_t[...], tqkv[:, first : first + cfg.C])
                        flat[:, part * cfg.C : (part + 1) * cfg.C] = value.astype(BF)
                reply = r.reply.at[layer, group]

                def write(first, rows, pair, value, reply=reply):
                    chunks, columns = pl.ds(first // SLOT, rows // SLOT), slice(pair * 128, pair * 128 + 128)
                    reply[chunks, :, columns] = value.astype(BF).reshape(rows // SLOT, SLOT, 128)

                attend(flat, r.kcol, r.krow, write)
                collect(cfg, me, reply, r.back.at[layer, group], sems.at[group, 2], sems.at[group, 3])

        if cfg.HS == 1:

            @pl.when(me >= cfg.ND)
            def _(left_t=left_t):
                left_t[...] = jnp.zeros(left_t.shape, BF)

        if layer + 1 < LAYERS:
            weights.load(layer + 1, "tqkv")
        save(left_t, r.o_left_t.at[layer])
        for group in range(cfg.HG):
            ends.append(functools.partial(collect_sent, cfg, me, r.reply.at[layer, group], sems.at[group, 2]))
            save(r.flat.at[layer, group], r.o_flat.at[layer, group])

        tproj = weights.get("tproj")
        for group in range(cfg.HG):
            wait_bytes(r.back.at[layer, group], sems.at[group, 3])
            for split in range(cfg.HS):
                first = head_columns(cfg, split, group)
                value = r.back[layer, group, split * cfg.G : (split + 1) * cfg.G]
                att[:, first : first + cfg.C] = value.reshape(cfg.R, cfg.C)
        proj[...] = dot(att[...], tproj[...]).astype(BF)
        tfc = weights.get("tfc")
        value = dot(proj[...], tfc[...])
        for rows in blocks:
            mid[rows, :] = x[rows, :] + jnp.where(patch_rows(cfg, rows), value[rows, :], 0.0)
        if layer + 1 < LAYERS:
            weights.load(layer + 1, "tproj", "tfc")
        save(mid, r.o_mid.at[layer])
        norm_forward(cfg, mid, r.norms[0, layer, 1:2, :], r.norms[1, layer, 1:2, :], n1)
        sqkv = weights.get("sqkv")
        qkv = r.qkv.at[layer]
        for first in range(0, 3 * cfg.D, cfg.D):
            qkv[:, first : first + cfg.D] = dot(n1[...], sqkv[:, first : first + cfg.D]).astype(BF)
        save(qkv, r.o_qkv.at[layer])

        def write(first, rows, pair, value, so=so):
            so[pl.ds(first, rows), pair * 128 : pair * 128 + 128] = value.astype(BF)

        attend(qkv, r.space_col, r.space_row, write)
        value = dot(so[...], weights.get("sproj")[...])
        after[...] = mid[...] + value
        if layer + 1 < LAYERS:
            weights.load(layer + 1, "sqkv", "sproj")
        save(after, r.o_after.at[layer])
        save(r.lefts.at[layer], r.o_lefts.at[layer])
        norm_forward(cfg, after, r.norms[0, layer, 2:3, :], r.norms[1, layer, 2:3, :], r.n2)
        full, part = r.full.at[layer], r.part.at[layer % 2]
        up, down = weights.get("up"), weights.get("down")

        def work(q, rows, full=full, part=part, up=up, down=down):
            for first in range(0, cfg.FW, 256):
                columns = slice(first, min(first + 256, cfg.FW))
                r.hidden[rows, columns] = gelu(dot(full[q, rows, :], up[:, columns])).astype(BF)
            part[q, rows, :] = dot(r.hidden[rows, :], down[...]).astype(BF)

        def write(rows, value, after=after, layer=layer):
            value = after[rows, :] + value
            if layer + 1 < LAYERS:
                r.x[layer + 1, rows, :] = value
            else:
                r.last[rows, :] = value.astype(BF)
                if rows.start == 0:
                    r.o_out_cls[...] = r.last[SLOT - 1 : SLOT, :]

        ends += exchange_tp(
            cfg,
            r.n2,
            full,
            part,
            r.from_mate.at[layer],
            r.from_across.at[layer],
            r.tp_sems.at[layer],
            work,
            lambda: None,
            lambda full=full, layer=layer: save(full, r.o_full.at[layer]),
            write,
        )
        if layer + 1 < LAYERS:
            weights.load(layer + 1, "up", "down")
            for wait in ends:
                wait()
            ends.clear()

    for copy in swaps_cot:
        copy.wait()
    for q in range(cfg.T):
        r.grad[q * own_rows : (q + 1) * own_rows, :] = r.cot_in[q].astype(F32)
    r.grad[SLOT - 1 : SLOT, :] = r.cot_cls[...].astype(F32)
    save(r.grad, r.o_grad)
    save(r.last, r.o_last)
    for wait in ends:
        wait()
    wait_bytes(r.keys.at[pl.ds(0, cfg.N - 1)], r.key_sems.at[0])
    for copy in saves:
        copy.wait()


def forward(cfg, arrays, cid):
    D, R, L = cfg.D, cfg.R, LAYERS
    rows_t, C3 = cfg.N * SLOT, 3 * cfg.C
    wide = D if cfg.HS == 1 else C3
    own_rows = R // cfg.T
    names = ["patches", "cots", "cls", "cot_cls", "norms"]
    inputs = {name: (arrays[name], VM) for name in names}
    inputs["clip"] = (arrays["clip"], pl.BlockSpec(memory_space=pltpu.SMEM))
    inputs |= {"w_" + name: (arrays["w_" + name], ANY) for name in WEIGHTS}
    outputs = dict(
        o_x=((L, R, D), F32, ANY),
        o_mid=((L, R, D), F32, ANY),
        o_after=((L, R, D), F32, ANY),
        o_lefts=((L, 4, R, D), BF, ANY),
        o_left_t=((L, left_rows(cfg), D), BF, ANY),
        o_flat=((L, cfg.HG, rows_t, C3), BF, ANY),
        o_qkv=((L, R, 3 * D), BF, ANY),
        o_full=((L, cfg.T, R, D), BF, ANY),
        o_kcol=((rows_t, 1), F32, ANY),
        o_krow=((1, rows_t), F32, ANY),
        o_grad=((R, D), F32, ANY),
        o_last=((R, D), BF, ANY),
        o_out_cls=((1, D), BF, VM),
    )
    scratch = weight_scratch(cfg) | dict(
        patch_in=pltpu.VMEM((cfg.T, own_rows, D), BF),
        cot_in=pltpu.VMEM((cfg.T, own_rows, D), BF),
        key=pltpu.VMEM((SLOT, 128), F32),
        space_col=pltpu.VMEM((R, 1), F32),
        space_row=pltpu.VMEM((1, R), F32),
        keys=pltpu.VMEM((cfg.N, SLOT, 128), F32),
        kcol=pltpu.VMEM((rows_t, 1), F32),
        krow=pltpu.VMEM((1, rows_t), F32),
        x=pltpu.VMEM((L, R, D), F32),
        mid=pltpu.VMEM((L, R, D), F32),
        after=pltpu.VMEM((L, R, D), F32),
        last=pltpu.VMEM((R, D), BF),
        grad=pltpu.VMEM((R, D), F32),
        lefts=pltpu.VMEM((L, 4, R, D), BF),
        left_t=pltpu.VMEM((L, left_rows(cfg), D), BF),
        sent=pltpu.VMEM((L, cfg.ND, SLOT, wide), BF),
        got=pltpu.VMEM((L, cfg.N, SLOT, wide), BF),
        flat=pltpu.VMEM((L, cfg.HG, rows_t, C3), BF),
        reply=pltpu.VMEM((L, cfg.HG, cfg.N, SLOT, cfg.C), BF),
        back=pltpu.VMEM((L, cfg.HG, cfg.ND, SLOT, cfg.C), BF),
        qkv=pltpu.VMEM((L, R, 3 * D), BF),
        n2=pltpu.VMEM((R, D), BF),
        hidden=pltpu.VMEM((R, cfg.FW), BF),
        full=pltpu.VMEM((L, cfg.T, R, D), BF),
        part=pltpu.VMEM((2, cfg.T, R, D), BF),
        from_mate=pltpu.VMEM((L, 2, R, D), BF),
        from_across=pltpu.VMEM((L, R, D), BF),
        w_sems=pltpu.SemaphoreType.DMA((len(WEIGHTS),)),
        swap_sems=pltpu.SemaphoreType.DMA((2, 2 * cfg.T)),
        key_sems=pltpu.SemaphoreType.DMA((2,)),
        time_sems=pltpu.SemaphoreType.DMA((L, cfg.HG, 4)),
        tp_sems=pltpu.SemaphoreType.DMA((L, 2, 12)),
        save_sems=pltpu.SemaphoreType.DMA((4 + L * (7 + cfg.HG),)),
    )
    def build(*args, **options):
        return pl.pallas_call(*args, **options)

    return call(build, forward_kernel, inputs, outputs, scratch, cid, cfg=cfg)


def reverse(index, bits):
    return sum(((index >> bit) & 1) << (bits - 1 - bit) for bit in range(bits))


def add(a, b):
    return (a.astype(F32) + b.astype(F32)).astype(BF)


class Pipe:
    def __init__(self, stages, partners, credits, total, slots, gaps, held, every):
        self.stages, self.partners, self.credits, self.total, self.every = stages, partners, credits, total, every
        self.slots, self.gaps, self.held = slots, gaps, held
        self.jobs, self.clock = [], 0
        self.done = [[] for _ in stages]
        self.last = len(stages) - 1

    def add_jobs(self, *jobs):
        self.jobs += jobs

    def ready(self, i, k):
        if i == 0:
            if k >= len(self.jobs) or (k >= self.held and len(self.done[1]) <= k - self.held):
                return False
            if k and self.clock - self.done[0][-1] < self.every:
                return False
        elif k >= len(self.done[i - 1]) or self.clock - self.done[i - 1][k] < self.gaps[i]:
            return False
        return i == self.last or k < self.slots or len(self.done[min(i + 2, self.last)]) > k - self.slots

    def tick(self):
        self.clock += 1
        for i in reversed(range(len(self.stages))):
            k = len(self.done[i])
            if not self.ready(i, k):
                continue
            if i < self.last and k >= self.slots:
                for at, _ in self.partners(i):
                    pl.semaphore_wait(self.credits.at[at], 1)
            self.stages[i](k, self.jobs[k])
            self.done[i].append(self.clock)
            if k + self.slots < self.total:
                for sender in range(self.last):
                    if min(sender + 2, self.last) == i:
                        for at, to in self.partners(sender):
                            pl.semaphore_signal(self.credits.at[at], inc=1, device_id=to, device_id_type=MESH)

    @property
    def open(self):
        return len(self.done[-1]) < len(self.jobs)


def attn_pipe(r, cfg, total, y_first):
    S, D, T = cfg.S, cfg.D, cfg.T
    bits = S.bit_length() - 1
    rows, half = D // S, D // 2
    seq, rank = lax.axis_index("seq"), lax.axis_index("tp")
    core, chip = rank % 2, rank // 2
    held, slots = r.partial.shape[0], r.core_in.shape[0]
    seq_in = [getattr(r, f"seq_in{bit}") for bit in range(bits)]

    def remote(source, target, i, k, **to):
        return pltpu.make_async_remote_copy(
            source, target, r.sends.at[i, k % slots], r.recvs.at[i, k % slots], device_id=to, device_id_type=MESH
        )

    def part(ref, bit, mine):
        size = S >> (bit + 1)
        own = (seq >> bit) % 2
        return ref.at[pl.ds((own if mine else 1 - own) * size, size)]

    def core_copy(k):
        return remote(r.partial.at[k % held, 1 - core], r.core_in.at[k % slots], 0, k, tp=rank ^ 1)

    def x_copy(k):
        if y_first:
            return remote(r.x_in.at[k % slots, :, 1 - chip], seq_in[0].at[k % slots], 2, k, tp=rank ^ 2)
        return remote(r.core_in.at[k % slots, :, 1 - chip], r.x_in.at[k % slots], 1, k, tp=rank ^ 2)

    def bit_copy(k, bit):
        to = {"seq": seq ^ (1 << bit)}
        if bit:
            return remote(part(seq_in[bit - 1].at[k % slots], bit, False), seq_in[bit].at[k % slots], 2 + bit, k, **to)
        if y_first:
            return remote(part(r.core_in.at[k % slots], 0, False), r.x_in.at[k % slots], 1, k, **to)
        return remote(part(r.x_in.at[k % slots], 0, False), seq_in[0].at[k % slots], 2, k, **to)

    def final_copy(k, i):
        ref = r.final.at[k % slots, rank]
        return remote(ref, ref, 1 + bits + i, k, tp=rank ^ i)

    def compute(k, job):
        left, right, _, _ = job
        for side in range(2):
            value = dot(left[...], right[:, side * half : side * half + half], TN).astype(BF)
            for s in range(S):
                r.partial[k % held, side, reverse(s, bits)] = value[s * rows : (s + 1) * rows].reshape(2, rows // 2, half)
        core_copy(k).start()

    def from_core(k, job):
        core_copy(k).wait()
        r.core_in[k % slots] = add(r.core_in[k % slots], r.partial[k % held, core])
        (bit_copy(k, 0) if y_first else x_copy(k)).start()

    def from_x(k, job):
        x_copy(k).wait()
        if y_first:
            seq_in[0][k % slots] = add(seq_in[0][k % slots], r.x_in[k % slots, :, chip])
            bit_copy(k, 1).start()
        else:
            r.x_in[k % slots] = add(r.x_in[k % slots], r.core_in[k % slots, :, chip])
            bit_copy(k, 0).start()

    def from_bit(k, job, bit):
        bit_copy(k, bit).wait()
        if bit:
            target, before = seq_in[bit], seq_in[bit - 1]
        elif y_first:
            target, before = r.x_in, r.core_in
        else:
            target, before = seq_in[0], r.x_in
        value = add(target[k % slots], part(before.at[k % slots], bit, True)[...])
        if bit < bits - 1:
            target[k % slots] = value
            (x_copy(k) if bit == 0 and y_first else bit_copy(k, bit + 1)).start()
        else:
            r.final[k % slots, rank] = value[0]
            for i in range(1, T):
                final_copy(k, i).start()

    def finish(k, job):
        _, _, layer, columns = job
        for i in range(1, T):
            final_copy(k, i).wait()
        if k >= 2:
            wait_bytes(r.attn_out.at[k % 2], r.out_sems.at[k % 2])
        for q in range(T):
            at = (q // 2) * (rows // 2)
            r.attn_out[k % 2, at : at + rows // 2, (q % 2) * half : (q % 2) * half + half] = r.final[k % slots, q]
        for column, first, size in columns:
            pltpu.make_async_copy(
                r.attn_out.at[k % 2, :, pl.ds(first, size)], r.o_attn.at[layer, :, pl.ds(column, size)], r.out_sems.at[k % 2]
            ).start()

    from_bits = [functools.partial(from_bit, bit=bit) for bit in range(bits)]
    if y_first:
        stages = [compute, from_core, from_bits[0], from_x, *from_bits[1:], finish]
    else:
        stages = [compute, from_core, from_x, *from_bits, finish]

    def partners(i):
        if i == 0:
            return [(i, {"tp": rank ^ 1})]
        if i == (2 if y_first else 1):
            return [(i, {"tp": rank ^ 2})]
        if i < 2 + bits:
            return [(i, {"seq": seq ^ (1 << max(i - 2, 0))})]
        return [(1 + bits + j, {"tp": rank ^ j}) for j in range(1, T)]

    gaps = [0, 2, 8, 8 if y_first else 6] + [5] * (bits - 1) + [5]
    pipe = Pipe(stages, partners, r.credits, total, slots, gaps, held, 2)

    def flush():
        for k in range(min(2, total)):
            wait_bytes(r.attn_out.at[k], r.out_sems.at[k])

    return pipe, flush


class Pipes:
    def __init__(self, pipes, turns):
        self.pipes, self.turns = pipes, list(turns)

    def add_jobs(self, *jobs):
        for job in jobs:
            self.pipes[self.turns.pop(0)].add_jobs(job)

    def tick(self):
        for pipe in self.pipes:
            pipe.tick()

    @property
    def open(self):
        return any(pipe.open for pipe in self.pipes)


PIPE_TAGS = ["x_", "y_"]
PIPE_REFS = ["partial", "core_in", "x_in", "final", "attn_out", "sends", "recvs", "credits", "out_sems"]


def pipe_refs(r, cfg, tag):
    names = PIPE_REFS + [f"seq_in{bit}" for bit in range(cfg.S.bit_length() - 1)]
    return SimpleNamespace(o_attn=r.o_attn, **{name: getattr(r, tag + name) for name in names})


def pipe_scratch(cfg, tag, held, slots, y_first):
    S, T, D = cfg.S, cfg.T, cfg.D
    bits = S.bit_length() - 1
    rows, half = D // S, D // 2
    small = (rows // 2, half)
    types = [
        pltpu.VMEM((held, 2, S, 2) + small, BF),
        pltpu.VMEM((slots, S, 2) + small, BF),
        pltpu.VMEM((slots,) + ((S // 2, 2) if y_first else (S,)) + small, BF),
        pltpu.VMEM((slots, T) + small, BF),
        pltpu.VMEM((2, rows, D), BF),
        pltpu.SemaphoreType.DMA((1 + bits + T, slots)),
        pltpu.SemaphoreType.DMA((1 + bits + T, slots)),
        pltpu.SemaphoreType.REGULAR((1 + bits + T,)),
        pltpu.SemaphoreType.DMA((2,)),
    ]
    scratch = {tag + name: kind for name, kind in zip(PIPE_REFS, types, strict=True)}
    for bit in range(bits):
        scratch[f"{tag}seq_in{bit}"] = pltpu.VMEM((slots, S >> (bit + 1)) + small, BF)
    return scratch


def pipe_turns(cfg):
    if (cfg.D // cfg.S // 2) % 16:
        return [0] * (9 * LAYERS)
    return [0, 0, 1] * (3 * LAYERS - 1) + [0, 1, 0]


def fc_pipe(r, cfg):
    S, D, T, R = cfg.S, cfg.D, cfg.T, cfg.R
    bits = S.bit_length() - 1
    rows = D // S
    width = r.fc_part.shape[-1]
    seq = lax.axis_index("seq")
    held, slots = r.fc_part.shape[0], r.fc_in0.shape[0]
    fc_in = [getattr(r, f"fc_in{bit}") for bit in range(bits)]

    def bit_copy(k, bit):
        source = r.fc_part.at[k % held] if bit == 0 else fc_in[bit - 1].at[k % slots]
        size = S >> (bit + 1)
        other = 1 - (seq >> bit) % 2
        return pltpu.make_async_remote_copy(
            source.at[pl.ds(other * size, size)],
            fc_in[bit].at[k % slots],
            r.fc_sends.at[bit, k % slots],
            r.fc_recvs.at[bit, k % slots],
            device_id={"seq": seq ^ (1 << bit)},
            device_id_type=MESH,
        )

    def compute(k, job):
        left, right, (place, column) = job
        value = dot(left[...].reshape(T * R, D), right[:, :, column : column + width].reshape(T * R, width), TN).astype(BF)
        for s in range(S):
            r.fc_part[k % held, reverse(s, bits)] = value[s * rows : (s + 1) * rows]
        bit_copy(k, 0).start()

    def from_bit(k, job, bit):
        _, _, (place, column) = job
        bit_copy(k, bit).wait()
        size = S >> (bit + 1)
        mine = pl.ds(((seq >> bit) % 2) * size, size)
        own = r.fc_part[k % held, mine] if bit == 0 else fc_in[bit - 1][k % slots, mine]
        if bit < bits - 1:
            fc_in[bit][k % slots] = add(fc_in[bit][k % slots], own)
            bit_copy(k, bit + 1).start()
        else:
            r.o_fc[place, :, column : column + width] = own[0].astype(F32) + fc_in[bit][k % slots, 0].astype(F32)

    stages = [compute] + [functools.partial(from_bit, bit=bit) for bit in range(bits)]


    def partners(i):
        return [(i, {"seq": seq ^ (1 << i)})]

    total = 2 * LAYERS * (cfg.FW // width)
    return Pipe(stages, partners, r.fc_credits, total, slots, [0] + [7] * bits, held, 1)


STATE = ["x", "mid", "after", "flat", "qkv", "full"]


def backward_kernel(r, cfg):
    D, R, T = cfg.D, cfg.R, cfg.T
    me = my_index(cfg)
    rows_t = cfg.N * SLOT
    C, C3 = cfg.C, 3 * cfg.C
    blocks = row_blocks(cfg)
    weights = Weights(r)
    state = {}

    def load(layer, *names):
        for name in names:
            copy = pltpu.make_async_copy(getattr(r, "i_" + name).at[layer], getattr(r, name), r.state_sems.at[STATE.index(name)])
            copy.start()
            state[name] = copy

    def get(name):
        if name in state:
            state.pop(name).wait()
        return getattr(r, name)

    top = LAYERS - 1
    load_grad = pltpu.make_async_copy(r.i_grad, r.grad, r.load_sems.at[0])
    load_lefts = pltpu.make_async_copy(r.i_lefts, r.lefts, r.load_sems.at[1])
    load_grad.start()
    load(top, "full")
    weights.load(top, "up", "down")
    load(top, "after")
    weights.load(top, "sproj")
    load(top, "qkv", "mid")
    load_lefts.start()
    load_left_t = pltpu.make_async_copy(r.i_left_t, r.left_t, r.load_sems.at[2])
    load_left_t.start()
    weights.load(top, "sqkv", "tfc", "tproj", "tqkv")
    load(top, "flat", "x")
    greet_all(cfg, me)
    r.space_col[...], r.space_row[...] = space_keys(cfg)
    out_swap = swap_tp(r.i_last, r.o_out, r.swap_sems.at[0])
    turns = pipe_turns(cfg)
    made = [attn_pipe(pipe_refs(r, cfg, tag), cfg, turns.count(i), i == 1) for i, tag in enumerate(PIPE_TAGS) if i in turns]
    attn = Pipes([pipe for pipe, _ in made], turns)
    fc = fc_pipe(r, cfg)
    loaded = []

    def beside(count):
        for _ in range(count):
            fc.tick()
            attn.tick()

    load_grad.wait()
    grad = r.grad
    for layer in reversed(range(LAYERS)):
        att, proj, n1, so = (r.lefts.at[layer, i] for i in range(4))
        dqkv_t, dqkv_s = r.dqkv_t.at[layer], r.dqkv_s.at[layer]
        gt1, gt2, gu = (r.rights.at[layer, i] for i in range(3))

        r.gm[...] = grad[...].astype(BF)
        full, up, down = get("full"), weights.get("up"), weights.get("down")

        def work(q, rows, full=full, up=up, down=down):
            for first in range(0, cfg.FW, 256):
                columns = slice(first, min(first + 256, cfg.FW))
                value = dot(full[q, rows, :], up[:, columns])
                cdf = 0.5 * (1.0 + lax.erf(value * 0.7071067811865476))
                slope = cdf + value * jnp.exp(-0.5 * value * value) * 0.3989422804014327
                back = dot(r.full_grad[q, rows, :], down[columns, :], NT)
                r.hidden[q, rows, columns] = (value * cdf).astype(BF)
                r.grad_pre[q, rows, columns] = (slope * back).astype(BF)
            r.part[q, rows, :] = dot(r.grad_pre[q, rows, :], up[...], NT).astype(BF)

        def last(layer=layer):
            width = r.fc_part.shape[-1]
            for column in range(0, cfg.FW, width):
                fc.add_jobs((r.full, r.grad_pre, (layer, column)), (r.full_grad, r.hidden, (LAYERS + layer, column)))
            beside(4)

        def write(rows, value):
            r.delta[rows, :] = value

        ends = exchange_tp(
            cfg,
            r.gm,
            r.full_grad,
            r.part,
            r.from_mate,
            r.from_across,
            r.tp_sems.at[layer],
            work,
            lambda: beside(1),
            last,
            write,
        )
        for wait in ends:
            wait()
        ends.clear()
        after = get("after")
        norm_backward(cfg, after, r.norms[0, layer, 2:3, :], lambda rows: r.delta[rows, :], grad, r.sums, layer, 2)
        gu[...] = grad[...].astype(BF)
        if not loaded:
            load_lefts.wait()
            load_left_t.wait()
            loaded.append(1)
        attn.add_jobs((so, gu, layer, [(8 * D, 0, D)]))
        beside(1)

        r.gso[...] = dot(gu[...], weights.get("sproj")[...], NT).astype(BF)
        beside(1)

        def write(first, rows, part, pair, value, dqkv_s=dqkv_s):
            start = part * D + pair * 128
            dqkv_s[pl.ds(first, rows), start : start + 128] = value.astype(BF)

        for pair in range(D // 128):
            attend_back(get("qkv"), r.gso, r.space_col, r.space_row, write, r.acc, [pair])
            beside(1)
        attn.add_jobs(*[(n1, dqkv_s.at[:, pl.ds(i * D, D)], layer, [((5 + i) * D, 0, D)]) for i in range(3)])
        sqkv = weights.get("sqkv")
        r.delta[...] = sum(dot(dqkv_s[:, i * D : i * D + D], sqkv[:, i * D : i * D + D], NT) for i in range(3))
        beside(1)
        norm_backward(cfg, get("mid"), r.norms[0, layer, 1:2, :], lambda rows: r.delta[rows, :], grad, r.sums, layer, 1)
        beside(1)

        for rows in blocks:
            gt2[rows, :] = jnp.where(patch_rows(cfg, rows), grad[rows, :], 0.0).astype(BF)
        gt1[...] = dot(gt2[...], weights.get("tfc")[...], NT).astype(BF)
        attn.add_jobs((proj, gt2, layer, [(4 * D, 0, D)]), (att, gt1, layer, [(3 * D, 0, D)]))
        beside(1)
        tproj = weights.get("tproj")
        sems = r.time_sems.at[layer]
        for group in range(cfg.HG):
            for split in range(cfg.HS):
                first = head_columns(cfg, split, group)
                value = dot(gt1[...], tproj[first : first + C, :], NT).astype(BF)
                r.sent[group, split * cfg.G : (split + 1) * cfg.G] = value.reshape(cfg.G, SLOT, C)
            spread(cfg, me, r.sent.at[group], r.got.at[group], sems.at[group, 0], sems.at[group, 1])
            ends.append(functools.partial(spread_sent, cfg, me, r.sent.at[group], sems.at[group, 0]))
            beside(1)
        flat, tqkv = get("flat"), weights.get("tqkv")
        for group in range(cfg.HG):

            def write(first, rows, part, pair, value, group=group, dqkv_t=dqkv_t):
                start = part * C + pair * 128
                if cfg.HS == 1:
                    start += group * C3
                    dqkv_t[pl.ds(first, rows), start : start + 128] = value.astype(BF)
                else:
                    chunks = pl.ds(first // SLOT, rows // SLOT)
                    r.reply[0, chunks, :, start : start + 128] = value.astype(BF).reshape(rows // SLOT, SLOT, 128)

            for pair in range(C // 128):

                @pl.when(me < cfg.ND)
                def _(group=group, sems=sems, pair=pair, write=write):
                    if pair == 0:
                        wait_bytes(r.got.at[group], sems.at[group, 1])
                        r.flat_grad[...] = r.got[group].reshape(rows_t, C)
                    attend_back(flat.at[group], r.flat_grad, r.kcol, r.krow, write, r.acc, [pair])

                beside(1)
            if cfg.HS == 1:

                @pl.when(me >= cfg.ND)
                def _(group=group, dqkv_t=dqkv_t):
                    dqkv_t[:, group * C3 : (group + 1) * C3] = jnp.zeros((rows_t, C3), BF)

                columns = [(part * D + group * C, part * C, C) for part in range(3)]
                attn.add_jobs((r.left_t.at[layer], dqkv_t.at[:, pl.ds(group * C3, C3)], layer, columns))

        for group in range(cfg.HG):

            @pl.when(me < cfg.ND)
            def _(group=group, sems=sems, dqkv_t=dqkv_t, tqkv=tqkv):
                if cfg.HS == 1:
                    rows = slice(group * C, (group + 1) * C)
                    value = sum(
                        dot(dqkv_t[:, g * C3 + i * C : g * C3 + (i + 1) * C], tqkv[rows, i * D + g * C : i * D + (g + 1) * C], NT)
                        for g in range(cfg.HG)
                        for i in range(3)
                    )
                    r.reply[group] = value.astype(BF).reshape(cfg.N, SLOT, C)
                collect(cfg, me, r.reply.at[group], r.back.at[group], sems.at[group, 2], sems.at[group, 3])

            ends.append(functools.partial(collect_sent, cfg, me, r.reply.at[group], sems.at[group, 2]))
            beside(1)
        if cfg.HS == 1:
            for group in range(cfg.HG):
                beside(1)
                wait_bytes(r.back.at[group], sems.at[group, 3])
                r.delta[:, group * C : (group + 1) * C] = r.back[group].reshape(R, C).astype(F32)
        else:
            wait_bytes(r.back.at[0], sems.at[0, 3])
            for split in range(cfg.HS):
                first = head_columns(cfg, split, 0)
                for part in range(3):
                    value = r.back[0, split * cfg.G : (split + 1) * cfg.G, :, part * C : (part + 1) * C]
                    dqkv_t[:, part * D + first : part * D + first + C] = value.reshape(R, C)
            attn.add_jobs(
                *[(r.left_t.at[layer], dqkv_t.at[:, pl.ds(i * D, D)], layer, [(i * D, 0, D)]) for i in range(3)]
            )
            r.delta[...] = sum(dot(dqkv_t[:, i * D : i * D + D], tqkv[:, i * D : i * D + D], NT) for i in range(3))
        beside(1)
        norm_backward(cfg, get("x"), r.norms[0, layer, 0:1, :], lambda rows: r.delta[rows, :], grad, r.sums, layer, 0)
        while len(fc.done[0]) < len(fc.jobs):
            beside(1)
        for wait in ends:
            wait()
        if layer:
            load(layer - 1, *STATE)
            weights.load(layer - 1, *WEIGHTS)

    rest = r.sums.shape[0] - 6 * LAYERS
    if rest:
        r.sums[6 * LAYERS :, :] = jnp.zeros((rest, D), F32)

    def window(seq):
        return pl.ds(pl.multiple_of(norm_window(cfg, seq), 128), r.norm_in.shape[2])

    def norm_copy(to):
        return send_copy(
            cfg, r.sums.at[:, window(to // T)], r.norm_in.at[me], r.norm_sems.at[0], r.norm_sems.at[1], to
        )

    to_all(cfg, me, norm_copy)
    pltpu.make_async_copy(r.sums.at[:, window(lax.axis_index("seq"))], r.norm_in.at[me], r.norm_sems.at[1]).start()
    own_rows = R // T
    for q in range(T):
        r.grad_out[q] = grad[q * own_rows : (q + 1) * own_rows, :].astype(BF)
    r.o_cls[...] = grad[SLOT - 1 : SLOT, :]
    grad_swap = swap_tp(r.grad_out, r.o_grad, r.swap_sems.at[1])
    while attn.open or fc.open:
        beside(1)
    for _, flush in made:
        flush()
    wait_bytes(r.norm_in, r.norm_sems.at[1])
    r.o_norm[...] = jnp.sum(r.norm_in[...], 0)
    wait_bytes(r.norm_in.at[pl.ds(0, cfg.N - 1)], r.norm_sems.at[0])
    for copy in out_swap + grad_swap:
        copy.wait()


def norm_window(cfg, seq):
    return jnp.minimum((seq * (cfg.D // cfg.S)) // 128 * 128, cfg.D - 256)


def backward(cfg, arrays, kept, cid):
    D, R, T, L, S, FW = cfg.D, cfg.R, cfg.T, LAYERS, cfg.S, cfg.FW
    rows_t, C, C3 = cfg.N * SLOT, cfg.C, 3 * cfg.C
    own_rows = R // T
    bits = S.bit_length() - 1
    rows = D // S
    width = FW // 2
    turns = pipe_turns(cfg)
    sizes, fc_held, fc_slots = ([(2, 5), (2, 4)], 2, 4) if 1 in turns else ([(1, 2)], 1, 2)
    inputs = dict(
        norms=(arrays["norms"], VM),
        kcol=(kept["o_kcol"], VM),
        krow=(kept["o_krow"], VM),
        i_last=(kept["last"], ANY),
        i_grad=(kept["o_grad"], ANY),
        i_lefts=(kept["o_lefts"], ANY),
        i_left_t=(kept["o_left_t"], ANY),
    )
    inputs |= {"i_" + name: (kept["o_" + name], ANY) for name in STATE}
    inputs |= {"w_" + name: (arrays["w_" + name], ANY) for name in WEIGHTS}
    outputs = dict(
        o_out=((T, own_rows, D), BF, ANY),
        o_grad=((T, own_rows, D), BF, ANY),
        o_cls=((1, D), F32, VM),
        o_attn=((L, rows, 9 * D), BF, ANY),
        o_fc=((2 * L, rows, FW), F32, VM),
        o_norm=((6 * L + -6 * L % 8, 256), F32, VM),
    )
    scratch = weight_scratch(cfg) | dict(
        space_col=pltpu.VMEM((R, 1), F32),
        space_row=pltpu.VMEM((1, R), F32),
        x=pltpu.VMEM((R, D), F32),
        mid=pltpu.VMEM((R, D), F32),
        after=pltpu.VMEM((R, D), F32),
        flat=pltpu.VMEM((cfg.HG, rows_t, C3), BF),
        qkv=pltpu.VMEM((R, 3 * D), BF),
        full=pltpu.VMEM((T, R, D), BF),
        grad=pltpu.VMEM((R, D), F32),
        delta=pltpu.VMEM((R, D), F32),
        lefts=pltpu.VMEM((L, 4, R, D), BF),
        left_t=pltpu.VMEM((L, left_rows(cfg), D), BF),
        rights=pltpu.VMEM((L, 3, R, D), BF),
        dqkv_t=pltpu.VMEM((L, left_rows(cfg), 3 * D), BF),
        dqkv_s=pltpu.VMEM((L, R, 3 * D), BF),
        gm=pltpu.VMEM((R, D), BF),
        gso=pltpu.VMEM((R, D), BF),
        full_grad=pltpu.VMEM((T, R, D), BF),
        hidden=pltpu.VMEM((T, R, FW), BF),
        grad_pre=pltpu.VMEM((T, R, FW), BF),
        part=pltpu.VMEM((T, R, D), BF),
        from_mate=pltpu.VMEM((2, R, D), BF),
        from_across=pltpu.VMEM((R, D), BF),
        sent=pltpu.VMEM((cfg.HG, cfg.ND, SLOT, C), BF),
        got=pltpu.VMEM((cfg.HG, cfg.N, SLOT, C), BF),
        flat_grad=pltpu.VMEM((rows_t, C), BF),
        reply=pltpu.VMEM((cfg.HG, cfg.N, SLOT, C if cfg.HS == 1 else C3), BF),
        back=pltpu.VMEM((cfg.HG, cfg.ND, SLOT, C if cfg.HS == 1 else C3), BF),
        acc=pltpu.VMEM((2, rows_t if rows_t > 256 else 8, 128), F32),
        sums=pltpu.VMEM((6 * L + -6 * L % 8, D), F32),
        norm_in=pltpu.VMEM((cfg.N, 6 * L + -6 * L % 8, 256), F32),
        grad_out=pltpu.VMEM((T, own_rows, D), BF),
        fc_part=pltpu.VMEM((fc_held, S, rows, width), BF),
        w_sems=pltpu.SemaphoreType.DMA((len(WEIGHTS),)),
        state_sems=pltpu.SemaphoreType.DMA((len(STATE),)),
        load_sems=pltpu.SemaphoreType.DMA((3,)),
        swap_sems=pltpu.SemaphoreType.DMA((2, 2 * T)),
        time_sems=pltpu.SemaphoreType.DMA((L, cfg.HG, 4)),
        tp_sems=pltpu.SemaphoreType.DMA((L, 2, 12)),
        fc_sends=pltpu.SemaphoreType.DMA((bits, fc_slots)),
        fc_recvs=pltpu.SemaphoreType.DMA((bits, fc_slots)),
        norm_sems=pltpu.SemaphoreType.DMA((2,)),
        fc_credits=pltpu.SemaphoreType.REGULAR((bits,)),
    )
    for bit in range(bits):
        scratch[f"fc_in{bit}"] = pltpu.VMEM((fc_slots, S >> (bit + 1), rows, width), BF)
    def build(*args, **options):
        return pl.pallas_call(*args, **options)

    for i, tag in enumerate(PIPE_TAGS):
        if i in turns:
            scratch |= pipe_scratch(cfg, tag, *sizes[i], i == 1)
    return call(build, backward_kernel, inputs, outputs, scratch, cid, cfg=cfg)


def shards(
    cfg,
    patches,
    cls_tokens,
    frame_clip,
    norm_gain,
    norm_bias,
    w_tqkv,
    w_tproj,
    w_tfc,
    w_sqkv,
    w_sproj,
    w_fc1,
    w_fc2,
    cot_patches,
    cot_cls,
):
    frames, local, D = patches.shape
    groups = local // cfg.PER
    def padded(x):
        x = x.reshape(frames, groups, cfg.PER, D)
        return jnp.pad(x, ((0, 0), (0, 0), (0, SLOT - cfg.PER), (0, 0))).reshape(frames, groups * SLOT, D)

    arrays = dict(
        patches=padded(patches),
        cots=padded(cot_patches),
        cls=cls_tokens,
        cot_cls=cot_cls,
        clip=frame_clip,
        norms=jnp.stack([norm_gain, norm_bias]),
        w_tqkv=w_tqkv,
        w_tproj=w_tproj,
        w_tfc=w_tfc,
        w_sqkv=w_sqkv,
        w_sproj=w_sproj,
        w_up=w_fc1,
        w_down=w_fc2,
    )
    kept = forward(cfg, arrays, 0)
    kept["last"] = kept["o_last"].reshape(cfg.T, -1, D)
    out = backward(cfg, arrays, kept, 1)

    def unpadded(x):
        return x.reshape(frames, groups, SLOT, D)[:, :, : cfg.PER].reshape(frames, local, D)

    rows = D // cfg.S
    seq = lax.axis_index("seq")
    norm = lax.dynamic_slice_in_dim(out["o_norm"][: 6 * LAYERS], seq * rows - norm_window(cfg, seq), rows, 1)
    fc = out["o_fc"]
    return (
        unpadded(out["o_out"]),
        kept["o_out_cls"],
        unpadded(out["o_grad"]).astype(F32),
        out["o_cls"],
        out["o_attn"].astype(F32),
        norm.reshape(LAYERS, 6, rows),
        fc[:LAYERS],
        jnp.swapaxes(fc[LAYERS:], 1, 2),
    )


def solution(mesh):
    S, T = mesh.shape["seq"], mesh.shape["tp"]

    def run(*args):
        local, D, FW = args[0].shape[1] // T, args[0].shape[2], args[10].shape[2] // T
        per = max(n for n in range(1, SLOT) if local % n == 0)
        groups = args[0].shape[1] // per
        pairs = D // (2 * HEAD_DIM)
        splits = max(n for n in range(1, pairs + 1) if pairs % n == 0 and (n == 1 or groups * n <= S * T))
        head_groups = 3 if splits == 1 and pairs % 3 == 0 else 1
        cfg = Cfg(
            S, T, S * T, D, groups, groups * SLOT, per, splits, groups * splits, head_groups, D // (splits * head_groups), FW
        )
        return jax.shard_map(
            functools.partial(shards, cfg),
            mesh=mesh,
            in_specs=(
                P("seq", "tp", None),
                P(("seq", "tp"), None),
                P("seq"),
                P(),
                P(),
                P(),
                P(),
                P(),
                P(),
                P(),
                P(None, None, "tp"),
                P(None, "tp", None),
                P("seq", "tp", None),
                P(("seq", "tp"), None),
            ),
            out_specs=(
                P("seq", "tp", None),
                P(("seq", "tp"), None),
                P("seq", "tp", None),
                P(("seq", "tp"), None),
                P(None, "seq", None),
                P(None, None, "seq"),
                P(None, "seq", "tp"),
                P(None, "tp", "seq"),
            ),
            check_vma=False,
        )(*args)

    return run
```

```python
import functools
from collections import namedtuple
from types import SimpleNamespace

import jax
import jax.numpy as jnp
from jax import lax
from jax.experimental import pallas as pl
from jax.experimental.pallas import tpu as pltpu
from jax.sharding import PartitionSpec as P

HEAD_DIM = 64
LAYERS = 2
SLOT = 8
EPS = 1e-06
NEG_FILL = -1e30
MESH = pl.DeviceIdType.MESH
BF = jnp.bfloat16
F32 = jnp.float32
NN = (((1,), (0,)), ((), ()))
NT = (((1,), (1,)), ((), ()))
TN = (((0,), (0,)), ((), ()))
VMEM_LIMIT = 62 * 1024 * 1024
BLOCK = 32

Cfg = namedtuple("Cfg", ["S", "T", "N", "D", "G", "R", "PER", "HS", "ND", "HG", "C", "FW"])


def dot(left, right, dims=NN):
    return lax.dot_general(left, right, dims, preferred_element_type=F32)


def params(cid=None):
    return pltpu.CompilerParams(
        collective_id=cid, has_side_effects=cid is not None, vmem_limit_bytes=VMEM_LIMIT
    )


ANY = pl.BlockSpec(memory_space=pl.ANY)
VM = pl.BlockSpec(memory_space=pltpu.VMEM)


def my_index(cfg):
    return lax.axis_index("seq") * cfg.T + lax.axis_index("tp")


def device(cfg, index):
    return (index // cfg.T, lax.rem(index, cfg.T))


def greet_all(cfg, me):
    barrier = pltpu.get_barrier_semaphore()

    def signal(i, carry):
        pl.semaphore_signal(
            barrier, inc=1, device_id=device(cfg, lax.rem(me + i, cfg.N)), device_id_type=MESH
        )
        return carry

    lax.fori_loop(1, cfg.N, signal, 0)
    pl.semaphore_wait(barrier, cfg.N - 1)


def wait_bytes(ref, sem):
    pltpu.make_async_copy(ref, ref, sem).wait()


def head_pair(ref, rows, width, part, pair):
    start = part * width + pair * 128
    return ref[rows, start : start + 128]


def weights_of(query, key, mask):
    scores = jnp.where(mask, dot(query, key, NT), NEG_FILL)
    top = jnp.max(scores, -1, keepdims=True)
    weight = jnp.exp(scores - top)
    return weight, jnp.sum(weight, -1, keepdims=True), top


def for_row_blocks(total, step, block):
    if total == step:
        block(0)
    else:

        def body(i, carry):
            block(pl.multiple_of(i * step, step))
            return carry

        lax.fori_loop(0, total // step, body, 0)


def attend(qkv, kcol, krow, write, lse, heads):
    total, width = qkv.shape[0], qkv.shape[1] // 3
    step = total if total <= 256 else 64
    every = slice(0, total)
    lane = lax.broadcasted_iota(jnp.int32, (step, 128), 1) < HEAD_DIM
    zero = jnp.zeros((), BF)

    def block(first):
        rows = pl.ds(first, step)
        mask = kcol[rows, :] == krow[...]
        for pair in range(width // 128):
            query = head_pair(qkv, rows, width, 0, pair) * jnp.asarray(HEAD_DIM**-0.5, BF)
            key = head_pair(qkv, every, width, 1, pair)
            value = head_pair(qkv, every, width, 2, pair)
            outs = []
            for half, own in enumerate((jnp.where(lane, query, zero), jnp.where(lane, zero, query))):
                weight, total_weight, top = weights_of(own, key, mask)
                outs.append(dot((weight * (1.0 / total_weight)).astype(BF), value))
                at = heads + 2 * pair + half
                lse[rows, at : at + 1] = top + jnp.log(total_weight)
            write(first, step, pair, jnp.where(lane, outs[0], outs[1]))

    for_row_blocks(total, step, block)


def attend_back(qkv, grad, kcol, krow, write, acc, pairs, lse, heads):
    total, width = qkv.shape[0], qkv.shape[1] // 3
    step = total if total <= 256 else 64
    every = slice(0, total)
    lane = lax.broadcasted_iota(jnp.int32, (step, 128), 1) < HEAD_DIM
    lane_all = lax.broadcasted_iota(jnp.int32, (total, 128), 1) < HEAD_DIM
    zero = jnp.zeros((), BF)
    scale = HEAD_DIM**-0.5

    for pair in pairs:

        def block(first, pair=pair):
            rows = pl.ds(first, step)
            mask = kcol[rows, :] == krow[...]
            key = head_pair(qkv, every, width, 1, pair)
            value = head_pair(qkv, every, width, 2, pair)
            query = head_pair(qkv, rows, width, 0, pair) * jnp.asarray(scale, BF)
            out = grad[rows, pair * 128 : pair * 128 + 128]
            dq, dk, dv = [], [], []
            for half in range(2):
                own = (lambda v: jnp.where(lane, zero, v)) if half else (lambda v: jnp.where(lane, v, zero))
                at = heads + 2 * pair + half
                prob = jnp.exp(jnp.where(mask, dot(own(query), key, NT), NEG_FILL) - lse[rows, at : at + 1])
                back = dot(own(out), value, NT)
                delta = jnp.sum(prob * back, -1, keepdims=True)
                score = (prob * (back - delta)).astype(BF)
                dq.append(dot(score, key))
                dk.append(dot(score, query, TN))
                dv.append(dot(prob.astype(BF), out, TN))
            write(first, step, 0, pair, jnp.where(lane, dq[0], dq[1]) * scale)
            grad_key, grad_value = jnp.where(lane_all, dk[0], dk[1]), jnp.where(lane_all, dv[0], dv[1])
            if total == step:
                write(0, total, 1, pair, grad_key)
                write(0, total, 2, pair, grad_value)
            else:
                acc[0] += grad_key
                acc[1] += grad_value

        if total > step:
            acc[...] = jnp.zeros(acc.shape, F32)
        for_row_blocks(total, step, block)
        if total > step:
            write(0, total, 1, pair, acc[0])
            write(0, total, 2, pair, acc[1])


def refs_by_name(names, refs):
    return SimpleNamespace(**dict(zip(names, refs, strict=True)))


def call(build, kernel, inputs, outputs, scratch, cid, **fixed):
    def body(*refs):
        kernel(refs_by_name([*inputs, *outputs, *scratch], refs), **fixed)

    results = build(
        body,
        out_shape=[jax.ShapeDtypeStruct(shape, dtype) for shape, dtype, _ in outputs.values()],
        in_specs=[spec for _, spec in inputs.values()],
        out_specs=[spec for _, _, spec in outputs.values()],
        scratch_shapes=list(scratch.values()),
        compiler_params=params(cid),
    )(*[array for array, _ in inputs.values()])
    return dict(zip(outputs, results, strict=True))


def row_blocks(cfg):
    return [slice(first, min(first + BLOCK, cfg.R)) for first in range(0, cfg.R, BLOCK)]


def normalize(x):
    center = x - jnp.mean(x, -1, keepdims=True)
    root = lax.rsqrt(jnp.mean(center * center, -1, keepdims=True) + EPS)
    return center * root, root


def norm_forward(cfg, src, gain, bias, out):
    for rows in row_blocks(cfg):
        value = (normalize(src[rows, :])[0] * gain + bias).astype(BF)
        if len(out.shape) == 2:
            out[rows, :] = value
        else:
            chunks = slice(rows.start // SLOT, rows.stop // SLOT)
            out[chunks] = value.reshape(chunks.stop - chunks.start, SLOT, cfg.D)


def norm_backward(cfg, src, gain, grad_of, total, sums, layer, which):
    by_gain = by_bias = None
    for rows in row_blocks(cfg):
        normal, root = normalize(src[rows, :])
        grad = grad_of(rows)
        scaled = grad * gain
        inner = jnp.mean(scaled * normal, -1, keepdims=True)
        total[rows, :] += root * (scaled - jnp.mean(scaled, -1, keepdims=True) - normal * inner)
        eights = (grad.shape[0] // 8, 8, grad.shape[1])
        one, two = jnp.sum((grad * normal).reshape(eights), 0), jnp.sum(grad.reshape(eights), 0)
        by_gain = one if by_gain is None else by_gain + one
        by_bias = two if by_bias is None else by_bias + two
    at = layer * 6 + which
    sums[at : at + 1, :] = jnp.sum(by_gain, 0, keepdims=True)
    sums[at + 3 : at + 4, :] = jnp.sum(by_bias, 0, keepdims=True)


def space_keys(cfg):
    row = lax.broadcasted_iota(jnp.int32, (1, cfg.R), 1)
    used = (lax.rem(row, SLOT) < cfg.PER) | (row == SLOT - 1)
    return jnp.zeros((cfg.R, 1), F32), jnp.where(used, 0.0, 1.0)


def patch_rows(cfg, rows):
    row = lax.broadcasted_iota(jnp.int32, (rows.stop - rows.start, 1), 0) + rows.start
    return lax.rem(row, SLOT) < cfg.PER


def to_all(cfg, me, copy_to, only=None):
    def send(i, carry):
        to = me ^ (cfg.N - i)
        if only is None:
            copy_to(to).start()
        else:

            @pl.when(to < only)
            def _():
                copy_to(to).start()

        return carry

    lax.fori_loop(1, cfg.N, send, 0)


def send_copy(cfg, src, dst, send, recv, to):
    return pltpu.make_async_remote_copy(src, dst, send, recv, device_id=device(cfg, to), device_id_type=MESH)


def tp_copy(src, dst, send, recv, rank):
    return pltpu.make_async_remote_copy(src, dst, send, recv, device_id={"tp": rank}, device_id_type=MESH)


def spread(cfg, me, src, dst, send, recv):
    to_all(cfg, me, lambda to: send_copy(cfg, src.at[to], dst.at[me], send, recv, to), cfg.ND)

    @pl.when(me < cfg.ND)
    def _():
        pltpu.make_async_copy(src.at[me], dst.at[me], recv).start()


def spread_sent(cfg, me, src, send):
    @pl.when(me < cfg.ND)
    def _():
        wait_bytes(src.at[pl.ds(0, cfg.ND - 1)], send)

    @pl.when(me >= cfg.ND)
    def _():
        wait_bytes(src, send)


def collect(cfg, me, src, dst, send, recv):
    to_all(cfg, me, lambda to: send_copy(cfg, src.at[to], dst.at[me], send, recv, to))
    pltpu.make_async_copy(src.at[me], dst.at[me], recv).start()


def collect_sent(cfg, me, src, send):
    @pl.when(me < cfg.ND)
    def _():
        wait_bytes(src.at[pl.ds(0, cfg.N - 1)], send)


def left_rows(cfg):
    return cfg.N * SLOT if cfg.HS == 1 else cfg.R


def head_columns(cfg, split, group):
    return (split * cfg.HG + group) * cfg.C


def swap_tp(x, out, sems):
    rank = lax.axis_index("tp")
    ranks = x.shape[0]
    local = pltpu.make_async_copy(x.at[rank], out.at[rank], sems.at[0])
    copies = [
        tp_copy(x.at[rank ^ i], out.at[rank], sems.at[i], sems.at[ranks + i], rank ^ i) for i in range(1, ranks)
    ]
    local.start()
    for copy in copies:
        copy.start()
    return [local, *copies]


def gelu(value):
    return 0.5 * value * (1.0 + lax.erf(value * 0.7071067811865476))


def gelu_slope(value):
    return 0.5 * (1.0 + lax.erf(value * 0.7071067811865476)) + value * jnp.exp(-0.5 * value * value) * 0.3989422804014327


def exchange_tp(cfg, own, full, part, from_mate, from_across, sems, work, beside, last, write):
    rank = lax.axis_index("tp")
    mate, across, far = rank ^ 1, rank ^ 2, rank ^ 3
    size = cfg.R // 2
    halves = [slice(0, size), slice(size, cfg.R)]

    def copies(h, rows):
        at = sems.at[h]
        return SimpleNamespace(
            across=tp_copy(own.at[rows], full.at[rank, rows], at.at[0], at.at[1], across),
            mate=tp_copy(own.at[rows], full.at[rank, rows], at.at[2], at.at[3], mate),
            forward=tp_copy(full.at[across, rows], full.at[across, rows], at.at[4], at.at[5], mate),
            first=tp_copy(part.at[far, rows], from_mate.at[0, rows], at.at[6], at.at[7], mate),
            second=tp_copy(part.at[mate, rows], from_mate.at[1, rows], at.at[8], at.at[9], mate),
            third=tp_copy(part.at[across, rows], from_across.at[rows], at.at[10], at.at[11], across),
        )

    both = [copies(h, rows) for h, rows in enumerate(halves)]
    for half in both:
        half.across.start()
        half.mate.start()
    full[rank] = own[...]
    for half, rows in zip(both, halves, strict=True):
        work(rank, rows)
        half.mate.wait_recv()
        work(mate, rows)
        beside()
    for half, rows in zip(both, halves, strict=True):
        half.across.wait_recv()
        half.forward.start()
        work(across, rows)
        half.forward.wait_recv()
        work(far, rows)
        half.first.start()
        half.second.start()
        beside()
        half.first.wait_recv()
        part[across, rows, :] = (part[across, rows, :].astype(F32) + from_mate[0, rows, :].astype(F32)).astype(BF)
        half.third.start()
    last()
    for half, rows in zip(both, halves, strict=True):
        half.second.wait_recv()
        half.third.wait_recv()
        near = part[rank, rows, :].astype(F32) + from_mate[1, rows, :].astype(F32)
        write(rows, near + from_across[rows, :].astype(F32))
    return [copy.wait_send for half in both for copy in vars(half).values()]


WEIGHTS = ["tqkv", "tproj", "tfc", "sqkv", "sproj", "up", "down"]


def weight_scratch(cfg):
    D, FW = cfg.D, cfg.FW
    shapes = [(D, 3 * D), (D, D), (D, D), (D, 3 * D), (D, D), (D, FW), (FW, D)]
    return {name: pltpu.VMEM(shape, BF) for name, shape in zip(WEIGHTS, shapes, strict=True)}


class Weights:
    def __init__(self, r):
        self.r, self.open = r, {}

    def load(self, layer, *names):
        for name in names:
            at = WEIGHTS.index(name)
            copy = pltpu.make_async_copy(getattr(self.r, "w_" + name).at[layer], getattr(self.r, name), self.r.w_sems.at[at])
            copy.start()
            self.open[name] = copy

    def get(self, name):
        if name in self.open:
            self.open.pop(name).wait()
        return getattr(self.r, name)


def forward_kernel(r, cfg):
    me = my_index(cfg)
    rank = lax.axis_index("tp")
    rows_t = cfg.N * SLOT
    C3 = 3 * cfg.C
    blocks = row_blocks(cfg)
    weights = Weights(r)
    weights.load(0, *WEIGHTS)
    greet_all(cfg, me)
    slot = lax.broadcasted_iota(jnp.int32, r.key.shape, 0)
    r.key[...] = (r.clip[rank] * SLOT + slot).astype(F32)
    r.space_col[...], r.space_row[...] = space_keys(cfg)
    swaps = swap_tp(r.patches, r.patch_in, r.swap_sems.at[0])
    swaps_cot = swap_tp(r.cots, r.cot_in, r.swap_sems.at[1])
    to_all(cfg, me, lambda to: send_copy(cfg, r.key, r.keys.at[me], r.key_sems.at[0], r.key_sems.at[1], to))
    pltpu.make_async_copy(r.key, r.keys.at[me], r.key_sems.at[1]).start()
    ends = []
    saves = []

    def save(src, dst):
        copy = pltpu.make_async_copy(src, dst, r.save_sems.at[len(saves)])
        copy.start()
        saves.append(copy)

    for copy in swaps:
        copy.wait()
    own_rows = cfg.R // cfg.T
    for q in range(cfg.T):
        r.x[0, q * own_rows : (q + 1) * own_rows, :] = r.patch_in[q].astype(F32)
    r.x[0, SLOT - 1 : SLOT, :] = r.cls[...].astype(F32)

    for layer in range(LAYERS):
        x, mid, after = r.x.at[layer], r.mid.at[layer], r.after.at[layer]
        att, proj, n1, so = (r.lefts.at[layer, i] for i in range(4))
        left_t = r.left_t.at[layer]
        save(x, r.o_x.at[layer])
        sems = r.time_sems.at[layer]
        gain0, bias0 = r.norms[0, layer, 0:1, :], r.norms[1, layer, 0:1, :]
        if cfg.HS == 1:
            sent = r.sent.at[layer]
            norm_forward(cfg, x, gain0, bias0, sent)
            spread(cfg, me, sent, r.got.at[layer], sems.at[0, 0], sems.at[0, 1])
            ends.append(functools.partial(spread_sent, cfg, me, sent, sems.at[0, 0]))
        else:
            norm_forward(cfg, x, gain0, bias0, left_t)
            tqkv = weights.get("tqkv")
            sent = r.sent.at[layer]
            for split in range(cfg.HS):
                first = head_columns(cfg, split, 0)
                for part in range(3):
                    value = dot(left_t[...], tqkv[:, part * cfg.D + first : part * cfg.D + first + cfg.C]).astype(BF)
                    sent[split * cfg.G : (split + 1) * cfg.G, :, part * cfg.C : (part + 1) * cfg.C] = value.reshape(
                        cfg.G, SLOT, cfg.C
                    )
            spread(cfg, me, sent, r.got.at[layer], sems.at[0, 0], sems.at[0, 1])
            ends.append(functools.partial(spread_sent, cfg, me, sent, sems.at[0, 0]))

        if layer == 0:
            wait_bytes(r.keys, r.key_sems.at[1])
            keys = r.keys[...].reshape(rows_t, 128)
            r.kcol[...] = keys[:, 0:1]
            r.krow[...] = jnp.transpose(keys)[0:1, :]
            save(r.kcol, r.o_kcol)
            save(r.krow, r.o_krow)

        tqkv = weights.get("tqkv")

        @pl.when(me < cfg.ND)
        def _(layer=layer, sems=sems, tqkv=tqkv, left_t=left_t):
            wait_bytes(r.got.at[layer], sems.at[0, 1])
            if cfg.HS == 1:
                left_t[...] = r.got[layer].reshape(rows_t, cfg.D)
            else:
                r.flat[layer, 0] = r.got[layer].reshape(rows_t, C3)
            for group in range(cfg.HG):
                flat = r.flat.at[layer, group]
                if cfg.HS == 1:
                    for part in range(3):
                        first = part * cfg.D + group * cfg.C
                        value = dot(left_t[...], tqkv[:, first : first + cfg.C])
                        flat[:, part * cfg.C : (part + 1) * cfg.C] = value.astype(BF)
                reply = r.reply.at[layer, group]

                def write(first, rows, pair, value, reply=reply):
                    chunks, columns = pl.ds(first // SLOT, rows // SLOT), slice(pair * 128, pair * 128 + 128)
                    reply[chunks, :, columns] = value.astype(BF).reshape(rows // SLOT, SLOT, 128)

                attend(flat, r.kcol, r.krow, write, r.lse_t.at[layer], group * (cfg.C // HEAD_DIM))
                collect(cfg, me, reply, r.back.at[layer, group], sems.at[group, 2], sems.at[group, 3])

        if cfg.HS == 1:

            @pl.when(me >= cfg.ND)
            def _(left_t=left_t):
                left_t[...] = jnp.zeros(left_t.shape, BF)

        if layer + 1 < LAYERS:
            weights.load(layer + 1, "tqkv")
        save(left_t, r.o_left_t.at[layer])
        save(r.lse_t.at[layer], r.o_lse_t.at[layer])
        for group in range(cfg.HG):
            ends.append(functools.partial(collect_sent, cfg, me, r.reply.at[layer, group], sems.at[group, 2]))
            save(r.flat.at[layer, group], r.o_flat.at[layer, group])

        tproj = weights.get("tproj")
        for group in range(cfg.HG):
            wait_bytes(r.back.at[layer, group], sems.at[group, 3])
            for split in range(cfg.HS):
                first = head_columns(cfg, split, group)
                value = r.back[layer, group, split * cfg.G : (split + 1) * cfg.G]
                att[:, first : first + cfg.C] = value.reshape(cfg.R, cfg.C)
        proj[...] = dot(att[...], tproj[...]).astype(BF)
        tfc = weights.get("tfc")
        value = dot(proj[...], tfc[...])
        for rows in blocks:
            mid[rows, :] = x[rows, :] + jnp.where(patch_rows(cfg, rows), value[rows, :], 0.0)
        if layer + 1 < LAYERS:
            weights.load(layer + 1, "tproj", "tfc")
        save(mid, r.o_mid.at[layer])
        norm_forward(cfg, mid, r.norms[0, layer, 1:2, :], r.norms[1, layer, 1:2, :], n1)
        sqkv = weights.get("sqkv")
        qkv = r.qkv.at[layer]
        for first in range(0, 3 * cfg.D, cfg.D):
            qkv[:, first : first + cfg.D] = dot(n1[...], sqkv[:, first : first + cfg.D]).astype(BF)
        save(qkv, r.o_qkv.at[layer])

        def write(first, rows, pair, value, so=so):
            so[pl.ds(first, rows), pair * 128 : pair * 128 + 128] = value.astype(BF)

        attend(qkv, r.space_col, r.space_row, write, r.lse_s.at[layer], 0)
        save(r.lse_s.at[layer], r.o_lse_s.at[layer])
        value = dot(so[...], weights.get("sproj")[...])
        after[...] = mid[...] + value
        if layer + 1 < LAYERS:
            weights.load(layer + 1, "sqkv", "sproj")
        save(after, r.o_after.at[layer])
        save(r.lefts.at[layer], r.o_lefts.at[layer])
        norm_forward(cfg, after, r.norms[0, layer, 2:3, :], r.norms[1, layer, 2:3, :], r.n2)
        full, part = r.full.at[layer], r.part.at[layer % 2]
        up, down = weights.get("up"), weights.get("down")

        def work(q, rows, full=full, part=part, up=up, down=down):
            for first in range(0, cfg.FW, 256):
                columns = slice(first, min(first + 256, cfg.FW))
                r.hidden[rows, columns] = gelu(dot(full[q, rows, :], up[:, columns])).astype(BF)
            part[q, rows, :] = dot(r.hidden[rows, :], down[...]).astype(BF)

        def write(rows, value, after=after, layer=layer):
            value = after[rows, :] + value
            if layer + 1 < LAYERS:
                r.x[layer + 1, rows, :] = value
            else:
                r.last[rows, :] = value.astype(BF)
                if rows.start == 0:
                    r.o_out_cls[...] = r.last[SLOT - 1 : SLOT, :]

        ends += exchange_tp(
            cfg,
            r.n2,
            full,
            part,
            r.from_mate.at[layer],
            r.from_across.at[layer],
            r.tp_sems.at[layer],
            work,
            lambda: None,
            lambda full=full, layer=layer: save(full, r.o_full.at[layer]),
            write,
        )
        if layer + 1 < LAYERS:
            weights.load(layer + 1, "up", "down")
            for wait in ends:
                wait()
            ends.clear()

    for copy in swaps_cot:
        copy.wait()
    for q in range(cfg.T):
        r.grad[q * own_rows : (q + 1) * own_rows, :] = r.cot_in[q].astype(F32)
    r.grad[SLOT - 1 : SLOT, :] = r.cot_cls[...].astype(F32)
    save(r.grad, r.o_grad)
    save(r.last, r.o_last)
    for wait in ends:
        wait()
    wait_bytes(r.keys.at[pl.ds(0, cfg.N - 1)], r.key_sems.at[0])
    for copy in saves:
        copy.wait()


def forward(cfg, arrays, cid):
    D, R, L = cfg.D, cfg.R, LAYERS
    rows_t, C3 = cfg.N * SLOT, 3 * cfg.C
    wide = D if cfg.HS == 1 else C3
    own_rows = R // cfg.T
    names = ["patches", "cots", "cls", "cot_cls", "norms"]
    inputs = {name: (arrays[name], VM) for name in names}
    inputs["clip"] = (arrays["clip"], pl.BlockSpec(memory_space=pltpu.SMEM))
    inputs |= {"w_" + name: (arrays["w_" + name], ANY) for name in WEIGHTS}
    outputs = dict(
        o_x=((L, R, D), F32, ANY),
        o_mid=((L, R, D), F32, ANY),
        o_after=((L, R, D), F32, ANY),
        o_lefts=((L, 4, R, D), BF, ANY),
        o_left_t=((L, left_rows(cfg), D), BF, ANY),
        o_lse_t=((L, rows_t, 128), F32, ANY),
        o_lse_s=((L, R, 128), F32, ANY),
        o_flat=((L, cfg.HG, rows_t, C3), BF, ANY),
        o_qkv=((L, R, 3 * D), BF, ANY),
        o_full=((L, cfg.T, R, D), BF, ANY),
        o_kcol=((rows_t, 1), F32, ANY),
        o_krow=((1, rows_t), F32, ANY),
        o_grad=((R, D), F32, ANY),
        o_last=((R, D), BF, ANY),
        o_out_cls=((1, D), BF, VM),
    )
    scratch = weight_scratch(cfg) | dict(
        patch_in=pltpu.VMEM((cfg.T, own_rows, D), BF),
        cot_in=pltpu.VMEM((cfg.T, own_rows, D), BF),
        key=pltpu.VMEM((SLOT, 128), F32),
        space_col=pltpu.VMEM((R, 1), F32),
        space_row=pltpu.VMEM((1, R), F32),
        keys=pltpu.VMEM((cfg.N, SLOT, 128), F32),
        kcol=pltpu.VMEM((rows_t, 1), F32),
        krow=pltpu.VMEM((1, rows_t), F32),
        x=pltpu.VMEM((L, R, D), F32),
        mid=pltpu.VMEM((L, R, D), F32),
        after=pltpu.VMEM((L, R, D), F32),
        last=pltpu.VMEM((R, D), BF),
        grad=pltpu.VMEM((R, D), F32),
        lefts=pltpu.VMEM((L, 4, R, D), BF),
        left_t=pltpu.VMEM((L, left_rows(cfg), D), BF),
        lse_t=pltpu.VMEM((L, rows_t, 128), F32),
        lse_s=pltpu.VMEM((L, R, 128), F32),
        sent=pltpu.VMEM((L, cfg.ND, SLOT, wide), BF),
        got=pltpu.VMEM((L, cfg.N, SLOT, wide), BF),
        flat=pltpu.VMEM((L, cfg.HG, rows_t, C3), BF),
        reply=pltpu.VMEM((L, cfg.HG, cfg.N, SLOT, cfg.C), BF),
        back=pltpu.VMEM((L, cfg.HG, cfg.ND, SLOT, cfg.C), BF),
        qkv=pltpu.VMEM((L, R, 3 * D), BF),
        n2=pltpu.VMEM((R, D), BF),
        hidden=pltpu.VMEM((R, cfg.FW), BF),
        full=pltpu.VMEM((L, cfg.T, R, D), BF),
        part=pltpu.VMEM((2, cfg.T, R, D), BF),
        from_mate=pltpu.VMEM((L, 2, R, D), BF),
        from_across=pltpu.VMEM((L, R, D), BF),
        w_sems=pltpu.SemaphoreType.DMA((len(WEIGHTS),)),
        swap_sems=pltpu.SemaphoreType.DMA((2, 2 * cfg.T)),
        key_sems=pltpu.SemaphoreType.DMA((2,)),
        time_sems=pltpu.SemaphoreType.DMA((L, cfg.HG, 4)),
        tp_sems=pltpu.SemaphoreType.DMA((L, 2, 12)),
        save_sems=pltpu.SemaphoreType.DMA((4 + L * (9 + cfg.HG),)),
    )
    def build(*args, **options):
        return pl.pallas_call(*args, **options)

    return call(build, forward_kernel, inputs, outputs, scratch, cid, cfg=cfg)


def reverse(index, bits):
    return sum(((index >> bit) & 1) << (bits - 1 - bit) for bit in range(bits))


def add(a, b):
    return (a.astype(F32) + b.astype(F32)).astype(BF)


class Pipe:
    def __init__(self, stages, partners, credits, total, slots, gaps, held, every):
        self.stages, self.partners, self.credits, self.total, self.every = stages, partners, credits, total, every
        self.slots, self.gaps, self.held = slots, gaps, held
        self.jobs, self.clock = [], 0
        self.done = [[] for _ in stages]
        self.last = len(stages) - 1

    def add_jobs(self, *jobs):
        self.jobs += jobs

    def ready(self, i, k):
        if i == 0:
            if k >= len(self.jobs) or (k >= self.held and len(self.done[1]) <= k - self.held):
                return False
            if k and self.clock - self.done[0][-1] < self.every:
                return False
        elif k >= len(self.done[i - 1]) or self.clock - self.done[i - 1][k] < self.gaps[i]:
            return False
        return i == self.last or k < self.slots or len(self.done[min(i + 2, self.last)]) > k - self.slots

    def tick(self):
        self.clock += 1
        for i in reversed(range(len(self.stages))):
            k = len(self.done[i])
            if not self.ready(i, k):
                continue
            if i < self.last and k >= self.slots:
                for at, _ in self.partners(i):
                    pl.semaphore_wait(self.credits.at[at], 1)
            self.stages[i](k, self.jobs[k])
            self.done[i].append(self.clock)
            if k + self.slots < self.total:
                for sender in range(self.last):
                    if min(sender + 2, self.last) == i:
                        for at, to in self.partners(sender):
                            pl.semaphore_signal(self.credits.at[at], inc=1, device_id=to, device_id_type=MESH)

    @property
    def open(self):
        return len(self.done[-1]) < len(self.jobs)


def attn_pipe(r, cfg, total, y_first):
    S, D, T = cfg.S, cfg.D, cfg.T
    bits = S.bit_length() - 1
    rows, half = D // S, D // 2
    seq, rank = lax.axis_index("seq"), lax.axis_index("tp")
    core, chip = rank % 2, rank // 2
    held, slots = r.partial.shape[0], r.core_in.shape[0]
    seq_in = [getattr(r, f"seq_in{bit}") for bit in range(bits)]

    def remote(source, target, i, k, **to):
        return pltpu.make_async_remote_copy(
            source, target, r.sends.at[i, k % slots], r.recvs.at[i, k % slots], device_id=to, device_id_type=MESH
        )

    def part(ref, bit, mine):
        size = S >> (bit + 1)
        own = (seq >> bit) % 2
        return ref.at[pl.ds((own if mine else 1 - own) * size, size)]

    def core_copy(k):
        return remote(r.partial.at[k % held, 1 - core], r.core_in.at[k % slots], 0, k, tp=rank ^ 1)

    def x_copy(k):
        if y_first:
            return remote(r.x_in.at[k % slots, :, 1 - chip], seq_in[0].at[k % slots], 2, k, tp=rank ^ 2)
        return remote(r.core_in.at[k % slots, :, 1 - chip], r.x_in.at[k % slots], 1, k, tp=rank ^ 2)

    def bit_copy(k, bit):
        to = {"seq": seq ^ (1 << bit)}
        if bit:
            return remote(part(seq_in[bit - 1].at[k % slots], bit, False), seq_in[bit].at[k % slots], 2 + bit, k, **to)
        if y_first:
            return remote(part(r.core_in.at[k % slots], 0, False), r.x_in.at[k % slots], 1, k, **to)
        return remote(part(r.x_in.at[k % slots], 0, False), seq_in[0].at[k % slots], 2, k, **to)

    def final_copy(k, i):
        ref = r.final.at[k % slots, rank]
        return remote(ref, ref, 1 + bits + i, k, tp=rank ^ i)

    def compute(k, job):
        left, right, _, _ = job
        for side in range(2):
            value = dot(left[...], right[:, side * half : side * half + half], TN).astype(BF)
            for s in range(S):
                r.partial[k % held, side, reverse(s, bits)] = value[s * rows : (s + 1) * rows].reshape(2, rows // 2, half)
        core_copy(k).start()

    def from_core(k, job):
        core_copy(k).wait()
        r.core_in[k % slots] = add(r.core_in[k % slots], r.partial[k % held, core])
        (bit_copy(k, 0) if y_first else x_copy(k)).start()

    def from_x(k, job):
        x_copy(k).wait()
        if y_first:
            seq_in[0][k % slots] = add(seq_in[0][k % slots], r.x_in[k % slots, :, chip])
            bit_copy(k, 1).start()
        else:
            r.x_in[k % slots] = add(r.x_in[k % slots], r.core_in[k % slots, :, chip])
            bit_copy(k, 0).start()

    def from_bit(k, job, bit):
        bit_copy(k, bit).wait()
        if bit:
            target, before = seq_in[bit], seq_in[bit - 1]
        elif y_first:
            target, before = r.x_in, r.core_in
        else:
            target, before = seq_in[0], r.x_in
        value = add(target[k % slots], part(before.at[k % slots], bit, True)[...])
        if bit < bits - 1:
            target[k % slots] = value
            (x_copy(k) if bit == 0 and y_first else bit_copy(k, bit + 1)).start()
        else:
            r.final[k % slots, rank] = value[0]
            for i in range(1, T):
                final_copy(k, i).start()

    def finish(k, job):
        _, _, layer, columns = job
        for i in range(1, T):
            final_copy(k, i).wait()
        if k >= 2:
            wait_bytes(r.attn_out.at[k % 2], r.out_sems.at[k % 2])
        for q in range(T):
            at = (q // 2) * (rows // 2)
            r.attn_out[k % 2, at : at + rows // 2, (q % 2) * half : (q % 2) * half + half] = r.final[k % slots, q]
        for column, first, size in columns:
            pltpu.make_async_copy(
                r.attn_out.at[k % 2, :, pl.ds(first, size)], r.o_attn.at[layer, :, pl.ds(column, size)], r.out_sems.at[k % 2]
            ).start()

    from_bits = [functools.partial(from_bit, bit=bit) for bit in range(bits)]
    if y_first:
        stages = [compute, from_core, from_bits[0], from_x, *from_bits[1:], finish]
    else:
        stages = [compute, from_core, from_x, *from_bits, finish]

    def partners(i):
        if i == 0:
            return [(i, {"tp": rank ^ 1})]
        if i == (2 if y_first else 1):
            return [(i, {"tp": rank ^ 2})]
        if i < 2 + bits:
            return [(i, {"seq": seq ^ (1 << max(i - 2, 0))})]
        return [(1 + bits + j, {"tp": rank ^ j}) for j in range(1, T)]

    gaps = [0, 2, 8, 8 if y_first else 6] + [5] * (bits - 1) + [5]
    pipe = Pipe(stages, partners, r.credits, total, slots, gaps, held, 2)

    def flush():
        for k in range(min(2, total)):
            wait_bytes(r.attn_out.at[k], r.out_sems.at[k])

    return pipe, flush


class Pipes:
    def __init__(self, pipes, turns):
        self.pipes, self.turns = pipes, list(turns)

    def add_jobs(self, *jobs):
        for job in jobs:
            self.pipes[self.turns.pop(0)].add_jobs(job)

    def tick(self):
        for pipe in self.pipes:
            pipe.tick()

    @property
    def open(self):
        return any(pipe.open for pipe in self.pipes)


PIPE_TAGS = ["x_", "y_"]
PIPE_REFS = ["partial", "core_in", "x_in", "final", "attn_out", "sends", "recvs", "credits", "out_sems"]


def pipe_refs(r, cfg, tag):
    names = PIPE_REFS + [f"seq_in{bit}" for bit in range(cfg.S.bit_length() - 1)]
    return SimpleNamespace(o_attn=r.o_attn, **{name: getattr(r, tag + name) for name in names})


def pipe_scratch(cfg, tag, held, slots, y_first):
    S, T, D = cfg.S, cfg.T, cfg.D
    bits = S.bit_length() - 1
    rows, half = D // S, D // 2
    small = (rows // 2, half)
    types = [
        pltpu.VMEM((held, 2, S, 2) + small, BF),
        pltpu.VMEM((slots, S, 2) + small, BF),
        pltpu.VMEM((slots,) + ((S // 2, 2) if y_first else (S,)) + small, BF),
        pltpu.VMEM((slots, T) + small, BF),
        pltpu.VMEM((2, rows, D), BF),
        pltpu.SemaphoreType.DMA((1 + bits + T, slots)),
        pltpu.SemaphoreType.DMA((1 + bits + T, slots)),
        pltpu.SemaphoreType.REGULAR((1 + bits + T,)),
        pltpu.SemaphoreType.DMA((2,)),
    ]
    scratch = {tag + name: kind for name, kind in zip(PIPE_REFS, types, strict=True)}
    for bit in range(bits):
        scratch[f"{tag}seq_in{bit}"] = pltpu.VMEM((slots, S >> (bit + 1)) + small, BF)
    return scratch


def pipe_turns(cfg):
    if (cfg.D // cfg.S // 2) % 16:
        return [0] * (9 * LAYERS)
    return [0, 0, 1] * (3 * LAYERS - 1) + [0, 1, 0]


def fc_pipe(r, cfg):
    S, D, T, R = cfg.S, cfg.D, cfg.T, cfg.R
    bits = S.bit_length() - 1
    rows = D // S
    width = r.fc_part.shape[-1]
    seq = lax.axis_index("seq")
    held, slots = r.fc_part.shape[0], r.fc_in0.shape[0]
    fc_in = [getattr(r, f"fc_in{bit}") for bit in range(bits)]

    def bit_copy(k, bit):
        source = r.fc_part.at[k % held] if bit == 0 else fc_in[bit - 1].at[k % slots]
        size = S >> (bit + 1)
        other = 1 - (seq >> bit) % 2
        return pltpu.make_async_remote_copy(
            source.at[pl.ds(other * size, size)],
            fc_in[bit].at[k % slots],
            r.fc_sends.at[bit, k % slots],
            r.fc_recvs.at[bit, k % slots],
            device_id={"seq": seq ^ (1 << bit)},
            device_id_type=MESH,
        )

    def compute(k, job):
        left, right, (place, column) = job
        value = dot(left[...].reshape(T * R, D), right[:, :, column : column + width].reshape(T * R, width), TN).astype(BF)
        for s in range(S):
            r.fc_part[k % held, reverse(s, bits)] = value[s * rows : (s + 1) * rows]
        bit_copy(k, 0).start()

    def from_bit(k, job, bit):
        _, _, (place, column) = job
        bit_copy(k, bit).wait()
        size = S >> (bit + 1)
        mine = pl.ds(((seq >> bit) % 2) * size, size)
        own = r.fc_part[k % held, mine] if bit == 0 else fc_in[bit - 1][k % slots, mine]
        if bit < bits - 1:
            fc_in[bit][k % slots] = add(fc_in[bit][k % slots], own)
            bit_copy(k, bit + 1).start()
        else:
            r.o_fc[place, :, column : column + width] = own[0].astype(F32) + fc_in[bit][k % slots, 0].astype(F32)

    stages = [compute] + [functools.partial(from_bit, bit=bit) for bit in range(bits)]


    def partners(i):
        return [(i, {"seq": seq ^ (1 << i)})]

    total = 2 * LAYERS * (cfg.FW // width)
    return Pipe(stages, partners, r.fc_credits, total, slots, [0] + [7] * bits, held, 1)


STATE = ["x", "mid", "after", "flat", "qkv", "full", "lse_t", "lse_s"]


def backward_kernel(r, cfg):
    D, R, T = cfg.D, cfg.R, cfg.T
    me = my_index(cfg)
    rows_t = cfg.N * SLOT
    C, C3 = cfg.C, 3 * cfg.C
    blocks = row_blocks(cfg)
    weights = Weights(r)
    state = {}

    def load(layer, *names):
        for name in names:
            copy = pltpu.make_async_copy(getattr(r, "i_" + name).at[layer], getattr(r, name), r.state_sems.at[STATE.index(name)])
            copy.start()
            state[name] = copy

    def get(name):
        if name in state:
            state.pop(name).wait()
        return getattr(r, name)

    top = LAYERS - 1
    load_grad = pltpu.make_async_copy(r.i_grad, r.grad, r.load_sems.at[0])
    load_lefts = pltpu.make_async_copy(r.i_lefts, r.lefts, r.load_sems.at[1])
    load_grad.start()
    load(top, "full")
    weights.load(top, "up", "down")
    load(top, "after")
    weights.load(top, "sproj")
    load(top, "qkv", "lse_s", "mid")
    load_lefts.start()
    load_left_t = pltpu.make_async_copy(r.i_left_t, r.left_t, r.load_sems.at[2])
    load_left_t.start()
    weights.load(top, "sqkv", "tfc", "tproj", "tqkv")
    load(top, "flat", "lse_t", "x")
    greet_all(cfg, me)
    r.space_col[...], r.space_row[...] = space_keys(cfg)
    out_swap = swap_tp(r.i_last, r.o_out, r.swap_sems.at[0])
    turns = pipe_turns(cfg)
    made = [attn_pipe(pipe_refs(r, cfg, tag), cfg, turns.count(i), i == 1) for i, tag in enumerate(PIPE_TAGS) if i in turns]
    attn = Pipes([pipe for pipe, _ in made], turns)
    fc = fc_pipe(r, cfg)
    loaded = []

    def beside(count):
        for _ in range(count):
            fc.tick()
            attn.tick()

    load_grad.wait()
    grad = r.grad
    for layer in reversed(range(LAYERS)):
        att, proj, n1, so = (r.lefts.at[layer, i] for i in range(4))
        dqkv_t, dqkv_s = r.dqkv_t.at[layer], r.dqkv_s.at[layer]
        gt1, gt2, gu = (r.rights.at[layer, i] for i in range(3))

        r.gm[...] = grad[...].astype(BF)
        full, up, down = get("full"), weights.get("up"), weights.get("down")

        def work(q, rows, full=full, up=up, down=down):
            for first in range(0, cfg.FW, 256):
                columns = slice(first, min(first + 256, cfg.FW))
                value = dot(full[q, rows, :], up[:, columns])
                cdf = 0.5 * (1.0 + lax.erf(value * 0.7071067811865476))
                slope = cdf + value * jnp.exp(-0.5 * value * value) * 0.3989422804014327
                back = dot(r.full_grad[q, rows, :], down[columns, :], NT)
                r.hidden[q, rows, columns] = (value * cdf).astype(BF)
                r.grad_pre[q, rows, columns] = (slope * back).astype(BF)
            r.part[q, rows, :] = dot(r.grad_pre[q, rows, :], up[...], NT).astype(BF)

        def last(layer=layer):
            width = r.fc_part.shape[-1]
            for column in range(0, cfg.FW, width):
                fc.add_jobs((r.full, r.grad_pre, (layer, column)), (r.full_grad, r.hidden, (LAYERS + layer, column)))
            beside(4)

        def write(rows, value):
            r.delta[rows, :] = value

        ends = exchange_tp(
            cfg,
            r.gm,
            r.full_grad,
            r.part,
            r.from_mate,
            r.from_across,
            r.tp_sems.at[layer],
            work,
            lambda: beside(1),
            last,
            write,
        )
        for wait in ends:
            wait()
        ends.clear()
        after = get("after")
        norm_backward(cfg, after, r.norms[0, layer, 2:3, :], lambda rows: r.delta[rows, :], grad, r.sums, layer, 2)
        gu[...] = grad[...].astype(BF)
        if not loaded:
            load_lefts.wait()
            load_left_t.wait()
            loaded.append(1)
        attn.add_jobs((so, gu, layer, [(8 * D, 0, D)]))
        beside(1)

        r.gso[...] = dot(gu[...], weights.get("sproj")[...], NT).astype(BF)
        beside(1)

        def write(first, rows, part, pair, value, dqkv_s=dqkv_s):
            start = part * D + pair * 128
            dqkv_s[pl.ds(first, rows), start : start + 128] = value.astype(BF)

        lse_s = get("lse_s")
        for pair in range(D // 128):
            attend_back(get("qkv"), r.gso, r.space_col, r.space_row, write, r.acc, [pair], lse_s, 0)
            beside(1)
        attn.add_jobs(*[(n1, dqkv_s.at[:, pl.ds(i * D, D)], layer, [((5 + i) * D, 0, D)]) for i in range(3)])
        sqkv = weights.get("sqkv")
        r.delta[...] = sum(dot(dqkv_s[:, i * D : i * D + D], sqkv[:, i * D : i * D + D], NT) for i in range(3))
        beside(1)
        norm_backward(cfg, get("mid"), r.norms[0, layer, 1:2, :], lambda rows: r.delta[rows, :], grad, r.sums, layer, 1)
        beside(1)

        for rows in blocks:
            gt2[rows, :] = jnp.where(patch_rows(cfg, rows), grad[rows, :], 0.0).astype(BF)
        gt1[...] = dot(gt2[...], weights.get("tfc")[...], NT).astype(BF)
        attn.add_jobs((proj, gt2, layer, [(4 * D, 0, D)]), (att, gt1, layer, [(3 * D, 0, D)]))
        beside(1)
        tproj = weights.get("tproj")
        sems = r.time_sems.at[layer]
        for group in range(cfg.HG):
            for split in range(cfg.HS):
                first = head_columns(cfg, split, group)
                value = dot(gt1[...], tproj[first : first + C, :], NT).astype(BF)
                r.sent[group, split * cfg.G : (split + 1) * cfg.G] = value.reshape(cfg.G, SLOT, C)
            spread(cfg, me, r.sent.at[group], r.got.at[group], sems.at[group, 0], sems.at[group, 1])
            ends.append(functools.partial(spread_sent, cfg, me, r.sent.at[group], sems.at[group, 0]))
            beside(1)
        flat, lse_t, tqkv = get("flat"), get("lse_t"), weights.get("tqkv")
        for group in range(cfg.HG):

            def write(first, rows, part, pair, value, group=group, dqkv_t=dqkv_t):
                start = part * C + pair * 128
                if cfg.HS == 1:
                    start += group * C3
                    dqkv_t[pl.ds(first, rows), start : start + 128] = value.astype(BF)
                else:
                    chunks = pl.ds(first // SLOT, rows // SLOT)
                    r.reply[0, chunks, :, start : start + 128] = value.astype(BF).reshape(rows // SLOT, SLOT, 128)

            for pair in range(C // 128):

                @pl.when(me < cfg.ND)
                def _(group=group, sems=sems, pair=pair, write=write):
                    if pair == 0:
                        wait_bytes(r.got.at[group], sems.at[group, 1])
                        r.flat_grad[...] = r.got[group].reshape(rows_t, C)
                    heads = group * (C // HEAD_DIM)
                    attend_back(flat.at[group], r.flat_grad, r.kcol, r.krow, write, r.acc, [pair], lse_t, heads)

                beside(1)
            if cfg.HS == 1:

                @pl.when(me >= cfg.ND)
                def _(group=group, dqkv_t=dqkv_t):
                    dqkv_t[:, group * C3 : (group + 1) * C3] = jnp.zeros((rows_t, C3), BF)

                columns = [(part * D + group * C, part * C, C) for part in range(3)]
                attn.add_jobs((r.left_t.at[layer], dqkv_t.at[:, pl.ds(group * C3, C3)], layer, columns))

        for group in range(cfg.HG):

            @pl.when(me < cfg.ND)
            def _(group=group, sems=sems, dqkv_t=dqkv_t, tqkv=tqkv):
                if cfg.HS == 1:
                    rows = slice(group * C, (group + 1) * C)
                    value = sum(
                        dot(dqkv_t[:, g * C3 + i * C : g * C3 + (i + 1) * C], tqkv[rows, i * D + g * C : i * D + (g + 1) * C], NT)
                        for g in range(cfg.HG)
                        for i in range(3)
                    )
                    r.reply[group] = value.astype(BF).reshape(cfg.N, SLOT, C)
                collect(cfg, me, r.reply.at[group], r.back.at[group], sems.at[group, 2], sems.at[group, 3])

            ends.append(functools.partial(collect_sent, cfg, me, r.reply.at[group], sems.at[group, 2]))
            beside(1)
        if cfg.HS == 1:
            for group in range(cfg.HG):
                beside(1)
                wait_bytes(r.back.at[group], sems.at[group, 3])
                r.delta[:, group * C : (group + 1) * C] = r.back[group].reshape(R, C).astype(F32)
        else:
            wait_bytes(r.back.at[0], sems.at[0, 3])
            for split in range(cfg.HS):
                first = head_columns(cfg, split, 0)
                for part in range(3):
                    value = r.back[0, split * cfg.G : (split + 1) * cfg.G, :, part * C : (part + 1) * C]
                    dqkv_t[:, part * D + first : part * D + first + C] = value.reshape(R, C)
            attn.add_jobs(
                *[(r.left_t.at[layer], dqkv_t.at[:, pl.ds(i * D, D)], layer, [(i * D, 0, D)]) for i in range(3)]
            )
            r.delta[...] = sum(dot(dqkv_t[:, i * D : i * D + D], tqkv[:, i * D : i * D + D], NT) for i in range(3))
        beside(1)
        norm_backward(cfg, get("x"), r.norms[0, layer, 0:1, :], lambda rows: r.delta[rows, :], grad, r.sums, layer, 0)
        while len(fc.done[0]) < len(fc.jobs):
            beside(1)
        for wait in ends:
            wait()
        if layer:
            load(layer - 1, *STATE)
            weights.load(layer - 1, *WEIGHTS)

    rest = r.sums.shape[0] - 6 * LAYERS
    if rest:
        r.sums[6 * LAYERS :, :] = jnp.zeros((rest, D), F32)

    def window(seq):
        return pl.ds(pl.multiple_of(norm_window(cfg, seq), 128), r.norm_in.shape[2])

    def norm_copy(to):
        return send_copy(
            cfg, r.sums.at[:, window(to // T)], r.norm_in.at[me], r.norm_sems.at[0], r.norm_sems.at[1], to
        )

    to_all(cfg, me, norm_copy)
    pltpu.make_async_copy(r.sums.at[:, window(lax.axis_index("seq"))], r.norm_in.at[me], r.norm_sems.at[1]).start()
    own_rows = R // T
    for q in range(T):
        r.grad_out[q] = grad[q * own_rows : (q + 1) * own_rows, :].astype(BF)
    r.o_cls[...] = grad[SLOT - 1 : SLOT, :]
    grad_swap = swap_tp(r.grad_out, r.o_grad, r.swap_sems.at[1])
    while attn.open or fc.open:
        beside(1)
    for _, flush in made:
        flush()
    wait_bytes(r.norm_in, r.norm_sems.at[1])
    r.o_norm[...] = jnp.sum(r.norm_in[...], 0)
    wait_bytes(r.norm_in.at[pl.ds(0, cfg.N - 1)], r.norm_sems.at[0])
    for copy in out_swap + grad_swap:
        copy.wait()


def norm_window(cfg, seq):
    return jnp.minimum((seq * (cfg.D // cfg.S)) // 128 * 128, cfg.D - 256)


def backward(cfg, arrays, kept, cid):
    D, R, T, L, S, FW = cfg.D, cfg.R, cfg.T, LAYERS, cfg.S, cfg.FW
    rows_t, C, C3 = cfg.N * SLOT, cfg.C, 3 * cfg.C
    own_rows = R // T
    bits = S.bit_length() - 1
    rows = D // S
    width = FW // 2
    turns = pipe_turns(cfg)
    sizes, fc_held, fc_slots = ([(2, 5), (2, 4)], 2, 4) if 1 in turns else ([(1, 2)], 1, 2)
    inputs = dict(
        norms=(arrays["norms"], VM),
        kcol=(kept["o_kcol"], VM),
        krow=(kept["o_krow"], VM),
        i_last=(kept["last"], ANY),
        i_grad=(kept["o_grad"], ANY),
        i_lefts=(kept["o_lefts"], ANY),
        i_left_t=(kept["o_left_t"], ANY),
    )
    inputs |= {"i_" + name: (kept["o_" + name], ANY) for name in STATE}
    inputs |= {"w_" + name: (arrays["w_" + name], ANY) for name in WEIGHTS}
    outputs = dict(
        o_out=((T, own_rows, D), BF, ANY),
        o_grad=((T, own_rows, D), BF, ANY),
        o_cls=((1, D), F32, VM),
        o_attn=((L, rows, 9 * D), BF, ANY),
        o_fc=((2 * L, rows, FW), F32, VM),
        o_norm=((6 * L + -6 * L % 8, 256), F32, VM),
    )
    scratch = weight_scratch(cfg) | dict(
        space_col=pltpu.VMEM((R, 1), F32),
        space_row=pltpu.VMEM((1, R), F32),
        x=pltpu.VMEM((R, D), F32),
        mid=pltpu.VMEM((R, D), F32),
        after=pltpu.VMEM((R, D), F32),
        flat=pltpu.VMEM((cfg.HG, rows_t, C3), BF),
        lse_t=pltpu.VMEM((rows_t, 128), F32),
        lse_s=pltpu.VMEM((R, 128), F32),
        qkv=pltpu.VMEM((R, 3 * D), BF),
        full=pltpu.VMEM((T, R, D), BF),
        grad=pltpu.VMEM((R, D), F32),
        delta=pltpu.VMEM((R, D), F32),
        lefts=pltpu.VMEM((L, 4, R, D), BF),
        left_t=pltpu.VMEM((L, left_rows(cfg), D), BF),
        rights=pltpu.VMEM((L, 3, R, D), BF),
        dqkv_t=pltpu.VMEM((L, left_rows(cfg), 3 * D), BF),
        dqkv_s=pltpu.VMEM((L, R, 3 * D), BF),
        gm=pltpu.VMEM((R, D), BF),
        gso=pltpu.VMEM((R, D), BF),
        full_grad=pltpu.VMEM((T, R, D), BF),
        hidden=pltpu.VMEM((T, R, FW), BF),
        grad_pre=pltpu.VMEM((T, R, FW), BF),
        part=pltpu.VMEM((T, R, D), BF),
        from_mate=pltpu.VMEM((2, R, D), BF),
        from_across=pltpu.VMEM((R, D), BF),
        sent=pltpu.VMEM((cfg.HG, cfg.ND, SLOT, C), BF),
        got=pltpu.VMEM((cfg.HG, cfg.N, SLOT, C), BF),
        flat_grad=pltpu.VMEM((rows_t, C), BF),
        reply=pltpu.VMEM((cfg.HG, cfg.N, SLOT, C if cfg.HS == 1 else C3), BF),
        back=pltpu.VMEM((cfg.HG, cfg.ND, SLOT, C if cfg.HS == 1 else C3), BF),
        acc=pltpu.VMEM((2, rows_t if rows_t > 256 else 8, 128), F32),
        sums=pltpu.VMEM((6 * L + -6 * L % 8, D), F32),
        norm_in=pltpu.VMEM((cfg.N, 6 * L + -6 * L % 8, 256), F32),
        grad_out=pltpu.VMEM((T, own_rows, D), BF),
        fc_part=pltpu.VMEM((fc_held, S, rows, width), BF),
        w_sems=pltpu.SemaphoreType.DMA((len(WEIGHTS),)),
        state_sems=pltpu.SemaphoreType.DMA((len(STATE),)),
        load_sems=pltpu.SemaphoreType.DMA((3,)),
        swap_sems=pltpu.SemaphoreType.DMA((2, 2 * T)),
        time_sems=pltpu.SemaphoreType.DMA((L, cfg.HG, 4)),
        tp_sems=pltpu.SemaphoreType.DMA((L, 2, 12)),
        fc_sends=pltpu.SemaphoreType.DMA((bits, fc_slots)),
        fc_recvs=pltpu.SemaphoreType.DMA((bits, fc_slots)),
        norm_sems=pltpu.SemaphoreType.DMA((2,)),
        fc_credits=pltpu.SemaphoreType.REGULAR((bits,)),
    )
    for bit in range(bits):
        scratch[f"fc_in{bit}"] = pltpu.VMEM((fc_slots, S >> (bit + 1), rows, width), BF)
    def build(*args, **options):
        return pl.pallas_call(*args, **options)

    for i, tag in enumerate(PIPE_TAGS):
        if i in turns:
            scratch |= pipe_scratch(cfg, tag, *sizes[i], i == 1)
    return call(build, backward_kernel, inputs, outputs, scratch, cid, cfg=cfg)


def shards(
    cfg,
    patches,
    cls_tokens,
    frame_clip,
    norm_gain,
    norm_bias,
    w_tqkv,
    w_tproj,
    w_tfc,
    w_sqkv,
    w_sproj,
    w_fc1,
    w_fc2,
    cot_patches,
    cot_cls,
):
    frames, local, D = patches.shape
    groups = local // cfg.PER
    def padded(x):
        x = x.reshape(frames, groups, cfg.PER, D)
        return jnp.pad(x, ((0, 0), (0, 0), (0, SLOT - cfg.PER), (0, 0))).reshape(frames, groups * SLOT, D)

    arrays = dict(
        patches=padded(patches),
        cots=padded(cot_patches),
        cls=cls_tokens,
        cot_cls=cot_cls,
        clip=frame_clip,
        norms=jnp.stack([norm_gain, norm_bias]),
        w_tqkv=w_tqkv,
        w_tproj=w_tproj,
        w_tfc=w_tfc,
        w_sqkv=w_sqkv,
        w_sproj=w_sproj,
        w_up=w_fc1,
        w_down=w_fc2,
    )
    kept = forward(cfg, arrays, 0)
    kept["last"] = kept["o_last"].reshape(cfg.T, -1, D)
    out = backward(cfg, arrays, kept, 1)

    def unpadded(x):
        return x.reshape(frames, groups, SLOT, D)[:, :, : cfg.PER].reshape(frames, local, D)

    rows = D // cfg.S
    seq = lax.axis_index("seq")
    norm = lax.dynamic_slice_in_dim(out["o_norm"][: 6 * LAYERS], seq * rows - norm_window(cfg, seq), rows, 1)
    fc = out["o_fc"]
    return (
        unpadded(out["o_out"]),
        kept["o_out_cls"],
        unpadded(out["o_grad"]).astype(F32),
        out["o_cls"],
        out["o_attn"].astype(F32),
        norm.reshape(LAYERS, 6, rows),
        fc[:LAYERS],
        jnp.swapaxes(fc[LAYERS:], 1, 2),
    )


def solution(mesh):
    S, T = mesh.shape["seq"], mesh.shape["tp"]

    def run(*args):
        local, D, FW = args[0].shape[1] // T, args[0].shape[2], args[10].shape[2] // T
        per = max(n for n in range(1, SLOT) if local % n == 0)
        groups = args[0].shape[1] // per
        pairs = D // (2 * HEAD_DIM)
        splits = max(n for n in range(1, pairs + 1) if pairs % n == 0 and (n == 1 or groups * n <= S * T))
        head_groups = 3 if splits == 1 and pairs % 3 == 0 else 1
        cfg = Cfg(
            S, T, S * T, D, groups, groups * SLOT, per, splits, groups * splits, head_groups, D // (splits * head_groups), FW
        )
        return jax.shard_map(
            functools.partial(shards, cfg),
            mesh=mesh,
            in_specs=(
                P("seq", "tp", None),
                P(("seq", "tp"), None),
                P("seq"),
                P(),
                P(),
                P(),
                P(),
                P(),
                P(),
                P(),
                P(None, None, "tp"),
                P(None, "tp", None),
                P("seq", "tp", None),
                P(("seq", "tp"), None),
            ),
            out_specs=(
                P("seq", "tp", None),
                P(("seq", "tp"), None),
                P("seq", "tp", None),
                P(("seq", "tp"), None),
                P(None, "seq", None),
                P(None, None, "seq"),
                P(None, "seq", "tp"),
                P(None, "tp", "seq"),
            ),
            check_vma=False,
        )(*args)

    return run
```
